128 devices in a mesh: grp: 2 (over y_hi), tp: 32 (over y_lo, x, z), rep: 2 (over core).
Axes of the slice: x: 4, y: 4 (y_hi: 2, y_lo: 2; y = y_hi * 2 + y_lo), z: 4, core: 2. Of those that a mesh axis runs over, the one named last changes fastest.
Arguments:
- hidden_states: bfloat16 [8, 8192], replicated, may hold values from -24 to 24
- attn_gain: float32 [8192], replicated, may hold values from 0.1 to 1.9
- ffn_gain: float32 [8192], replicated, may hold values from 0.1 to 1.9
- w_query: bfloat16 [8192, 2, 32, 128], P('grp', 'rep', 'tp'), may hold values from -0.0625 to 0.0625
- w_keyval: bfloat16 [8192, 2, 1024], P('grp', 'rep', 'tp'), may hold values from -0.0625 to 0.0625
- w_out: bfloat16 [2, 32, 128, 8192], P('rep', 'tp', None, 'grp'), may hold values from -0.0625 to 0.0625
- w_gate: bfloat16 [8192, 14336], P('grp', ('tp', 'rep')), may hold values from -0.0625 to 0.0625
- w_up: bfloat16 [8192, 14336], P('grp', ('tp', 'rep')), may hold values from -0.0625 to 0.0625
- w_down: bfloat16 [14336, 8192], P(('tp', 'rep'), 'grp'), may hold values from -0.125 to 0.125
- kv_cache: bfloat16 [8, 32768, 8, 256], P(None, ('grp', 'tp'), 'rep'), may hold values from -70 to 70
- lengths: int32 [8], replicated, may hold values from 1 to 32768, as said below
- first_shard: int32 [8], replicated, may hold values from 0 to 63
Outputs:
- layer_out: bfloat16 [8, 8192], P(None, ('grp', 'tp', 'rep'))
The draws below stay inside these ranges and needn't reach their ends.
Inputs may be any that keep to these rules, and one draw needn't show every extreme that they name: `lengths`: some request has exactly 32768 cached tokens in every draw.
All inputs are finite; a program needn't handle non-finite values.
Results may differ from the reference program's by a relative error of at most 0.025.
Values may be sent and summed in bfloat16 or wider, within the bound.
A program may use at most 128 MiB of HBM per device.

```python
import math
import jax
import jax.numpy as jnp
from jax import lax

D = 8192
H = 64
KVH = 8
HD = 128
FF = 14336
REQS = 8
CTX_DEV = 512
CTX = 32768
N_GRP = 2
N_TP = 32
N_REP = 2


def draw_hidden_states(key, part):
    key = jax.random.fold_in(key, 3)
    key_base = jax.random.fold_in(key, 0)
    base = jnp.clip(jax.random.normal(key_base, (REQS, D), jnp.float32), -6.0, 6.0)
    return base.astype(jnp.bfloat16)


def draw_kv_cache(key, part):
    key = jax.random.fold_in(key, 7)
    key_keys, key_values = jax.random.split(key, 2)
    shape = (REQS, CTX, KVH, HD)
    key_part = jnp.clip(2.5 * jax.random.normal(key_keys, shape, jnp.float32), -15.0, 15.0)
    value_part = jnp.clip(jax.random.normal(key_values, shape, jnp.float32), -6.0, 6.0)
    return jnp.concatenate((key_part, value_part), axis=-1).astype(jnp.bfloat16)


def draw_lengths(key, part):
    key = jax.random.fold_in(key, 5)
    key_exp, key_len, key_pick = jax.random.split(key, 3)
    exponent = jax.random.randint(key_exp, (REQS,), 0, 17)
    ceiling = jnp.minimum(jnp.left_shift(jnp.ones((REQS,), jnp.int32), exponent), CTX)
    drawn = 1 + jax.random.randint(key_len, (REQS,), 0, ceiling)
    chosen = jax.random.randint(key_pick, (), 0, REQS)
    return jnp.where(jnp.arange(REQS) == chosen, CTX, drawn).astype(jnp.int32)


def touch_ends(result, rng, smallest, high):
    longest = result.shape.index(max(result.shape))
    spots = []
    for shift in (0, 1):
        where = [jax.random.randint(jax.random.fold_in(rng, axis), (), 0, length) for axis, length in enumerate(result.shape)]
        where[longest] = (where[longest] + shift) % result.shape[longest]
        spots.append(tuple(where))
    return result.at[spots[0]].set(smallest).at[spots[1]].set(high)


def strengthened(values, own_key, source, target, parts, factor):
    def block_of(dim):
        return (jnp.arange(values.shape[dim]) // (values.shape[dim] // parts)).reshape((-1,) + (1,) * (values.ndim - 1 - dim))

    near = jax.random.permutation(own_key, parts)[block_of(target)]
    other_side = (block_of(target) + parts // 2) % parts
    return jnp.where((block_of(source) == near) | (block_of(source) == other_side), factor * values, values)


def level_of(own_key, shape, cuts, smallest, high):
    def one(axis_at, shards_of):
        draws = jax.random.uniform(jax.random.fold_in(jax.random.fold_in(own_key, 6), axis_at), (shards_of,), jnp.float32, smallest / len(cuts), high / len(cuts))
        return jnp.repeat(jnp.exp(draws), shape[axis_at] // shards_of).reshape((-1,) + (1,) * (len(shape) - axis_at - 1))

    level = one(*cuts[0])
    for cut in cuts[1:]:
        level = level * one(*cut)
    return level


def centred(key, shape, width, most, shards=(), held_as=jnp.bfloat16):
    array = width * jax.random.normal(key, shape, jnp.float32)
    if shards:
        array = array * level_of(key, shape, shards, -0.22, 0.18)
    return jnp.clip(array, -most, most).astype(held_as)


def noise_with(own_key, extent, scale, bound, cuts, heavy, kind=jnp.bfloat16):
    values = scale * jax.random.normal(own_key, extent, jnp.float32)
    if cuts:
        values = values * level_of(own_key, extent, cuts, -0.22, 0.18)
    return jnp.clip(strengthened(values, jax.random.fold_in(own_key, 3), *heavy), -bound, bound).astype(kind)


def setup_inputs(seed: int = 0) -> dict:
    keys = jax.random.split(jax.random.key(seed), 13)
    return {
        "hidden_states": draw_hidden_states(jax.random.fold_in(keys[12], 71), 0),
        "attn_gain": jnp.clip(1.0 + 0.18 * jax.random.normal(keys[1], (D,), jnp.float32), 0.1, 1.9),
        "ffn_gain": jnp.clip(1.0 + 0.18 * jax.random.normal(keys[2], (D,), jnp.float32), 0.1, 1.9),
        "w_query": centred(keys[3], (D, N_REP, H // N_REP, HD), D ** -0.5, 0.0625, ((0, 2), (1, 2), (2, 32))),
        "w_keyval": centred(keys[4], (D, N_REP, (KVH // N_REP) * 2 * HD), D ** -0.5, 0.0625, ((0, 2), (1, 2), (2, 32))),
        "w_out": centred(keys[5], (N_REP, H // N_REP, HD, D), (H * HD) ** -0.5, 0.0625, ((0, 2), (1, 32), (3, 2))),
        "w_gate": centred(keys[6], (D, FF), D ** -0.5, 0.0625, ((0, 2), (1, 64))),
        "w_up": centred(keys[7], (D, FF), D ** -0.5, 0.0625, ((0, 2), (1, 64))),
        "w_down": noise_with(keys[8], (FF, D), FF ** -0.5, 0.125, ((0, 64), (1, 2)), (0, 1, 64, 4.0)),
        "kv_cache": draw_kv_cache(jax.random.fold_in(keys[12], 71), 0),
        "lengths": draw_lengths(jax.random.fold_in(keys[12], 71), 0),
        "first_shard": touch_ends(jax.random.randint(keys[11], (REQS,), 0, N_GRP * N_TP), jax.random.fold_in(keys[11], 1), 0, (N_GRP * N_TP) - 1).astype(jnp.int32),
    }


epsilon = 1e-05
base_freq = 500000.0
masked = -1e+30

def scaled_norm(values_in, gain):
    return values_in * lax.rsqrt(lax.optimization_barrier(jnp.mean(values_in * values_in, axis=-1, keepdims=True)) + epsilon) * gain

def rotary(pairs_in, positions):
    head_width = pairs_in.shape[-1]
    frequency = base_freq ** (-(2.0 * jnp.arange(head_width // 2, dtype=jnp.float32)) / head_width)
    angles = positions.astype(jnp.float32)[:, None] * frequency[None, :]
    cos_part = jnp.cos(angles)[:, None, :]
    sin_part = jnp.sin(angles)[:, None, :]
    halves = pairs_in.reshape(pairs_in.shape[:-1] + (head_width // 2, 2))
    real_part = halves[..., 0]
    imag_part = halves[..., 1]
    turned = jnp.stack((real_part * cos_part - imag_part * sin_part, real_part * sin_part + imag_part * cos_part), axis=-1)
    return turned.reshape(pairs_in.shape)

def reference(hidden_states, attn_gain, ffn_gain, w_query, w_keyval, w_out, w_gate, w_up, w_down, kv_cache, lengths, first_shard):
    states = hidden_states.astype(jnp.float32)
    normed = scaled_norm(states, attn_gain).astype(jnp.bfloat16)
    query = jnp.dot(normed, w_query.reshape(D, H * HD), preferred_element_type=jnp.float32).astype(jnp.bfloat16)
    keyval = jnp.dot(normed, w_keyval.reshape(D, KVH * 2 * HD), preferred_element_type=jnp.float32).astype(jnp.bfloat16)
    keyval = keyval.reshape(REQS, KVH, 2 * HD)
    query_rot = rotary(query.astype(jnp.float32).reshape(REQS, H, HD), lengths).astype(jnp.bfloat16)
    key_rot = rotary(keyval[:, :, :HD].astype(jnp.float32), lengths).astype(jnp.bfloat16)
    new_value = keyval[:, :, HD:].astype(jnp.float32)
    slot_index = jnp.arange(CTX, dtype=jnp.int32)
    block_total = N_GRP * N_TP
    position = ((slot_index // CTX_DEV)[None, :] - first_shard[:, None]) % block_total * CTX_DEV + (slot_index % CTX_DEV)[None, :]
    live_slot = position < lengths[:, None]
    group_size = H // KVH
    inv_scale = 1.0 / math.sqrt(HD)
    outputs = []
    for kv_index in range(KVH):
        q_block = query_rot[:, kv_index * group_size:(kv_index + 1) * group_size].astype(jnp.float32)
        cached_keys = kv_cache[:, :, kv_index, :HD].astype(jnp.float32)
        cached_values = kv_cache[:, :, kv_index, HD:].astype(jnp.float32)
        scores = jnp.einsum('bgd,bcd->bgc', q_block, cached_keys) * inv_scale
        scores = jnp.where(live_slot[:, None, :], scores, masked)
        own_score = jnp.einsum('bgd,bd->bg', q_block, key_rot[:, kv_index].astype(jnp.float32)) * inv_scale
        peak_score = jnp.maximum(lax.optimization_barrier(jnp.max(scores, axis=-1)), own_score)
        weights = jnp.where(live_slot[:, None, :], jnp.exp(scores - peak_score[..., None]), 0.0)
        own_weight = jnp.exp(own_score - peak_score)
        denominator = lax.optimization_barrier(jnp.sum(weights, axis=-1)) + own_weight
        rounded = lax.optimization_barrier(weights.astype(jnp.bfloat16)).astype(jnp.float32)
        own_rounded = lax.optimization_barrier(own_weight.astype(jnp.bfloat16)).astype(jnp.float32)
        numerator = jnp.einsum('bgc,bcd->bgd', rounded, cached_values)
        numerator = numerator + own_rounded[..., None] * new_value[:, kv_index][:, None, :]
        outputs.append(numerator / denominator[..., None])
    attended = jnp.concatenate(outputs, axis=1).astype(jnp.bfloat16).reshape(REQS, H * HD)
    projected = jnp.dot(attended, w_out.reshape(H * HD, D), preferred_element_type=jnp.float32)
    middle = (states + projected).astype(jnp.bfloat16)
    normed_ffn = scaled_norm(middle.astype(jnp.float32), ffn_gain).astype(jnp.bfloat16)
    gate_term = jnp.dot(normed_ffn, w_gate, preferred_element_type=jnp.float32)
    up_term = jnp.dot(normed_ffn, w_up, preferred_element_type=jnp.float32)
    hidden = (jax.nn.silu(gate_term) * up_term).astype(jnp.bfloat16)
    down_term = jnp.dot(hidden, w_down, preferred_element_type=jnp.float32)
    return (middle.astype(jnp.float32) + down_term).astype(jnp.bfloat16)
```

```python
import functools
import math

import numpy as np
import jax
import jax.numpy as jnp
from jax import lax
from jax.sharding import PartitionSpec as P
import jax.experimental.pallas as pl
import jax.experimental.pallas.tpu as pltpu

MESH = pl.DeviceIdType.MESH
NT = (((1,), (1,)), ((), ()))
epsilon = 1e-05
base_freq = 500000.0
masked = -1e30
floor_peak = -1e20

REQ = 8
WIDTH = 8192
HALF = WIDTH // 2
TILES = HALF // 128
HD = 128
CTX_DEV = 512
HEADS = 32
N_TP = 32
PEERS = 64
UNITS = 224
FREQ = [
    float(f)
    for f in (base_freq ** (-(2.0 * np.arange(HD // 2, dtype=np.float64)) / HD)).astype(np.float32)
]


def swap_halves(tile, diagonal):
    turned = pltpu.roll(pltpu.roll(tile, 64, 1), 4, 0)
    return jnp.where(diagonal, tile, turned)


def layer(
    hidden_ref, attn_gain_ref, ffn_gain_ref, wq_ref, wkv_ref, wo_ref, wg_ref, wu_ref, wd_ref,
    kv_ref, len_ref, first_ref, out_ref,
    hid, gain_a, gain_f, wq, wkv, wo, wg, wu, wd, keys, values,
    send_a, recv_a, q_rot, stage_c, send_c, recv_c, send_d, recv_d, recv_e, send_f, recv_f,
    send_g, recv_g, x_ffn, load_sem, kv_sem, send_sem, recv_sem,
):
    g = lax.axis_index("grp")
    t = lax.axis_index("tp")
    r = lax.axis_index("rep")
    me_row = g * N_TP + t
    me_col = t * 2 + r

    def row_peer(k):
        p = (me_row + k) % PEERS
        return p, (p // N_TP, p % N_TP, r)

    def col_peer(k):
        p = (me_col + k) % PEERS
        return p, (g, p // 2, p % 2)

    own_half = pl.ds(pl.multiple_of(g * HALF, HALF), HALF)
    other_half = pl.ds(pl.multiple_of((1 - g) * HALF, HALF), HALF)
    loads = [
        (hidden_ref.at[:, own_half], hid.at[0]),
        (hidden_ref.at[:, other_half], hid.at[1]),
        (attn_gain_ref.at[:, own_half], gain_a),
        (wq_ref, wq),
        (wkv_ref, wkv),
        (ffn_gain_ref.at[:, own_half], gain_f),
        (wo_ref, wo),
        (wg_ref, wg),
        (wu_ref, wu),
        (wd_ref, wd),
    ]
    copies = [pltpu.make_async_copy(s, d, load_sem.at[i]) for i, (s, d) in enumerate(loads)]
    kv_copies = []
    for b in range(REQ):
        for i, dst in enumerate((keys, values)):
            kv_copies.append(
                pltpu.make_async_copy(
                    kv_ref.at[b, :, :, pl.ds(i * HD, HD)], dst.at[b], kv_sem.at[2 * b + i]
                )
            )
    for c in copies[:6] + kv_copies + copies[6:]:
        c.start()

    barrier = pltpu.get_barrier_semaphore()

    @pl.loop(1, PEERS)
    def _(k):
        _, dev = row_peer(k)
        pl.semaphore_signal(barrier, inc=1, device_id=dev, device_id_type=MESH)

    pl.semaphore_signal(barrier, inc=1, device_id=(g, t, 1 - r), device_id_type=MESH)

    for c in copies[:5]:
        c.wait()
    own = hid[0].astype(jnp.float32)
    other = hid[1].astype(jnp.float32)
    squares = jnp.sum(own * own, axis=1, keepdims=True) + jnp.sum(
        other * other, axis=1, keepdims=True
    )
    scale = lax.rsqrt(squares * (1.0 / WIDTH) + epsilon)
    normed = (own * scale * gain_a[...]).astype(jnp.bfloat16)
    query_part = jnp.dot(normed, wq[...], preferred_element_type=jnp.float32)
    keyval_part = lax.dot_general(normed, wkv[...], NT, preferred_element_type=jnp.float32)
    keyval_wide = jnp.concatenate(
        (keyval_part, jnp.zeros((REQ, HD - 32), jnp.float32)), axis=1
    )
    spot = t % 4
    placed = keyval_wide
    for s in range(1, 4):
        placed = jnp.where(spot == s, pltpu.roll(keyval_wide, 32 * s, 1), placed)
    message = jnp.concatenate((query_part, placed), axis=0).astype(jnp.bfloat16)
    send_a[...] = message
    recv_a[me_row] = message

    pl.semaphore_wait(barrier, PEERS)

    def send_all(peer, source, landing, stage):
        @pl.loop(1, PEERS)
        def _(k):
            p, dev = peer(k)
            pltpu.make_async_remote_copy(
                src_ref=source(p),
                dst_ref=landing,
                send_sem=send_sem.at[stage],
                recv_sem=recv_sem.at[stage],
                device_id=dev,
                device_id_type=MESH,
            ).start()

    def wait_all(buffer, sem):
        span = buffer.at[pl.ds(0, PEERS - 1)]
        pltpu.make_async_copy(span, span, sem).wait()

    send_all(row_peer, lambda p: send_a, recv_a.at[me_row], 0)

    lane8 = lax.broadcasted_iota(jnp.int32, (REQ, HD), 1)
    row8 = lax.broadcasted_iota(jnp.int32, (REQ, HD), 0)
    frequency = jnp.zeros((REQ, HD), jnp.float32)
    for i in range(HD // 2):
        frequency = jnp.where(lane8 // 2 == i, FREQ[i], frequency)
    position = jnp.zeros((REQ, HD), jnp.int32)
    for b in range(REQ):
        position = jnp.where(row8 == b, len_ref[b], position)
    angles = position.astype(jnp.float32) * frequency
    cos_part = jnp.cos(angles)
    sin_part = jnp.sin(angles)
    even = lane8 % 2 == 0
    sin_even = jnp.where(even, -sin_part, 0.0)
    sin_odd = jnp.where(even, 0.0, sin_part)

    def rotate(x):
        return (
            x * cos_part + pltpu.roll(x, HD - 1, 1) * sin_even + pltpu.roll(x, 1, 1) * sin_odd
        )

    rounded = lambda x: x.astype(jnp.bfloat16).astype(jnp.float32)
    lane_r = lax.broadcasted_iota(jnp.int32, (HEADS, 4 * CTX_DEV), 1)
    head_r = lax.broadcasted_iota(jnp.int32, (HEADS, 4 * CTX_DEV), 0)
    wrong_head = (lane_r % 4) != (head_r // 8)
    slot_lane = jnp.where(wrong_head, 4 * CTX_DEV, lane_r)
    lane_c = lax.broadcasted_iota(jnp.int32, (HEADS, HD), 1)
    diagonal = (lane8 < 64) == (row8 < 4)
    inv_scale = 1.0 / math.sqrt(HD)

    wait_all(recv_a, recv_sem.at[0])
    for head in range(HEADS):
        pair = recv_a[head].astype(jnp.float32) + recv_a[N_TP + head].astype(jnp.float32)
        q_rot[pl.ds(head * REQ, REQ), :] = rounded(rotate(rounded(pair[:REQ])))

    for b in range(REQ):
        kv_copies[2 * b].wait()
        kv_copies[2 * b + 1].wait()
        block = (me_row - first_ref[b]) & (PEERS - 1)
        live_rows = 4 * (len_ref[b] - block * CTX_DEV)
        q_b = q_rot[pl.ds(b, HEADS, stride=REQ), :].astype(jnp.bfloat16)
        k_b = keys[b].reshape(4 * CTX_DEV, HD)
        v_b = values[b].reshape(4 * CTX_DEV, HD)
        scores = lax.dot_general(q_b, k_b, NT, preferred_element_type=jnp.float32)
        scores = jnp.where(slot_lane < jnp.minimum(live_rows, 4 * CTX_DEV), scores * inv_scale, masked)
        peak = jnp.maximum(jnp.max(scores, axis=1, keepdims=True), floor_peak)
        peak_hi = rounded(peak)
        peak_lo = rounded(peak - peak_hi)
        weights = jnp.exp(scores - (peak_hi + peak_lo))
        total = jnp.sum(weights, axis=1, keepdims=True)
        total_hi = rounded(total)
        total_lo = rounded(total - total_hi)
        numerator = jnp.dot(weights.astype(jnp.bfloat16), v_b, preferred_element_type=jnp.float32)
        stats = jnp.where(
            lane_c < 64,
            jnp.where(lane_c < 32, peak_hi, peak_lo),
            jnp.where(lane_c < 96, total_hi, total_lo),
        )
        stage_c[pl.ds(b, HEADS, stride=16), :] = numerator
        stage_c[pl.ds(REQ + b, HEADS, stride=16), :] = stats
    for head in range(HEADS):
        send_c[head] = stage_c[pl.ds(head * 16, 16), :].astype(jnp.bfloat16)
    recv_c[me_row] = send_c[t]
    send_all(row_peer, lambda p: send_c.at[p % N_TP], recv_c.at[me_row], 1)

    kv_first = (t // 8) * 8
    new_key = jnp.zeros((REQ, HD), jnp.float32)
    new_value = jnp.zeros((REQ, HD), jnp.float32)
    for j in range(4):
        part = recv_a[kv_first + j].astype(jnp.float32) + recv_a[N_TP + kv_first + j].astype(
            jnp.float32
        )
        new_key = new_key + part[REQ:]
        part = recv_a[kv_first + 4 + j].astype(jnp.float32) + recv_a[
            N_TP + kv_first + 4 + j
        ].astype(jnp.float32)
        new_value = new_value + part[REQ:]
    key_rot = rounded(rotate(rounded(new_key)))
    new_value = rounded(new_value)
    my_query = q_rot[pl.ds(pl.multiple_of(t * REQ, REQ), REQ), :]
    own_score = jnp.sum(my_query * key_rot, axis=1, keepdims=True) * inv_scale
    pick_row = lax.broadcasted_iota(jnp.int32, (HD, 2 * HD), 0)
    pick_col = lax.broadcasted_iota(jnp.int32, (HD, 2 * HD), 1)
    pick = jnp.where(
        (pick_row % 32 == 0) & (pick_row // 64 == pick_col // HD), 1.0, 0.0
    ).astype(jnp.bfloat16)

    wait_all(recv_c, recv_sem.at[1])
    partial = recv_c[...]
    stats_all = partial.astype(jnp.float32)[:, REQ:, :].reshape(PEERS * REQ, HD).astype(jnp.bfloat16)
    spread = jnp.dot(stats_all, pick, preferred_element_type=jnp.float32)
    peaks = spread[:, :HD].reshape(PEERS, REQ, HD)
    totals = spread[:, HD:].reshape(PEERS, REQ, HD)
    top = jnp.maximum(jnp.max(peaks, axis=0), own_score)
    keep = jnp.exp(peaks - top[None])
    own_weight = jnp.exp(own_score - top)
    numer = jnp.sum(keep * partial.astype(jnp.float32)[:, :REQ, :], axis=0)
    denom = jnp.sum(keep * totals, axis=0) + own_weight
    attended = ((numer + rounded(own_weight) * new_value) / denom).astype(jnp.bfloat16)

    def scatter(send, recv, row, weight, stage):
        for i in range(TILES // 2):
            product = jnp.dot(
                row, weight[:, pl.ds(i * 256, 256)], preferred_element_type=jnp.float32
            )
            for j in range(2):
                tile = swap_halves(product[:, j * 128 : j * 128 + 128], diagonal)
                send[4 * i + 2 * j] = tile[:4]
                send[4 * i + 2 * j + 1] = tile[4:]
        recv[me_col] = send[me_col]
        send_all(col_peer, lambda p: send.at[p], recv.at[me_col], stage)

    copies[6].wait()
    scatter(send_d, recv_d, attended, wo, 2)
    my_column = pl.ds(pl.multiple_of(t * 128, 128), 128)
    my_hidden = swap_halves(hid[0, :, my_column].astype(jnp.float32), diagonal)
    my_hidden = jnp.where(r == 0, my_hidden[:4], my_hidden[4:])
    wait_all(recv_d, recv_sem.at[2])
    projected = jnp.sum(recv_d[...], axis=0)
    recv_e[me_col] = projected
    send_all(col_peer, lambda p: recv_e.at[me_col], recv_e.at[me_col], 3)
    my_middle = rounded(my_hidden + projected)
    for c in copies[5:6] + copies[7:]:
        c.wait()
    wait_all(recv_e, recv_sem.at[3])
    squares = jnp.zeros((REQ, HD), jnp.float32)
    for i in range(TILES):
        packed = jnp.concatenate((recv_e[2 * i], recv_e[2 * i + 1]), axis=0)
        col = pl.ds(i * 128, 128)
        middle = rounded(hid[0, :, col].astype(jnp.float32) + swap_halves(packed, diagonal))
        squares = squares + middle * middle
        x_ffn[:, col] = (middle * gain_f[:, col]).astype(jnp.bfloat16)

    x = x_ffn[...]
    gate_part = lax.dot_general(x, wg[...], NT, preferred_element_type=jnp.float32)
    up_part = lax.dot_general(x, wu[...], NT, preferred_element_type=jnp.float32)
    square_sum = jnp.broadcast_to(jnp.sum(squares, axis=1, keepdims=True), (REQ, 256 - UNITS))
    send_f[0] = jnp.concatenate((gate_part, square_sum), axis=1)
    send_f[1] = jnp.concatenate((up_part, square_sum), axis=1)
    swap = pltpu.make_async_remote_copy(
        src_ref=send_f,
        dst_ref=recv_f,
        send_sem=send_sem.at[4],
        recv_sem=recv_sem.at[4],
        device_id=(1 - g, t, r),
        device_id_type=MESH,
    )
    swap.start()
    swap.wait_recv()
    gate_sum = send_f[0] + recv_f[0]
    up_sum = send_f[1] + recv_f[1]
    scale = lax.rsqrt(gate_sum[:, UNITS : UNITS + 1] * (1.0 / WIDTH) + epsilon)
    gate = gate_sum[:, :UNITS] * scale
    up = up_sum[:, :UNITS] * scale
    active = (gate / (1.0 + jnp.exp(-gate)) * up).astype(jnp.bfloat16)

    scatter(send_g, recv_g, active, wd, 5)
    wait_all(recv_g, recv_sem.at[5])
    result = my_middle + jnp.sum(recv_g[...], axis=0)
    out_ref[...] = jnp.concatenate((result[:, :64], result[:, 64:]), axis=0).astype(out_ref.dtype)

    wait_all(recv_a, send_sem.at[0])
    wait_all(recv_c, send_sem.at[1])
    wait_all(recv_d, send_sem.at[2])
    wait_all(recv_e, send_sem.at[3])
    swap.wait_send()
    wait_all(recv_g, send_sem.at[5])


def on_device(
    hidden_states, attn_gain, ffn_gain, w_query, w_keyval, w_out, w_gate, w_up, w_down,
    kv_cache, lengths, first_shard,
):
    anywhere = pl.BlockSpec(memory_space=pl.ANY)
    scalars = pl.BlockSpec(memory_space=pltpu.SMEM)
    f32, bf16 = jnp.float32, jnp.bfloat16
    return pl.pallas_call(
        layer,
        out_shape=jax.ShapeDtypeStruct((REQ, 64), bf16),
        in_specs=[anywhere] * 10 + [scalars] * 2,
        out_specs=pl.BlockSpec(memory_space=pltpu.VMEM),
        scratch_shapes=[
            pltpu.VMEM((2, REQ, HALF), bf16),
            pltpu.VMEM((1, HALF), f32),
            pltpu.VMEM((1, HALF), f32),
            pltpu.VMEM((HALF, HD), bf16),
            pltpu.VMEM((32, HALF), bf16),
            pltpu.VMEM((HD, HALF), bf16),
            pltpu.VMEM((UNITS, HALF), bf16),
            pltpu.VMEM((UNITS, HALF), bf16),
            pltpu.VMEM((UNITS, HALF), bf16),
            pltpu.VMEM((REQ, CTX_DEV, 4, HD), bf16),
            pltpu.VMEM((REQ, CTX_DEV, 4, HD), bf16),
            pltpu.VMEM((16, HD), bf16),
            pltpu.VMEM((PEERS, 16, HD), bf16),
            pltpu.VMEM((HEADS * REQ, HD), f32),
            pltpu.VMEM((HEADS * 16, HD), f32),
            pltpu.VMEM((HEADS, 16, HD), bf16),
            pltpu.VMEM((PEERS, 16, HD), bf16),
            pltpu.VMEM((PEERS, 4, HD), f32),
            pltpu.VMEM((PEERS, 4, HD), f32),
            pltpu.VMEM((PEERS, 4, HD), f32),
            pltpu.VMEM((2, REQ, 256), f32),
            pltpu.VMEM((2, REQ, 256), f32),
            pltpu.VMEM((PEERS, 4, HD), f32),
            pltpu.VMEM((PEERS, 4, HD), f32),
            pltpu.VMEM((REQ, HALF), bf16),
            pltpu.SemaphoreType.DMA((10,)),
            pltpu.SemaphoreType.DMA((2 * REQ,)),
            pltpu.SemaphoreType.DMA((6,)),
            pltpu.SemaphoreType.DMA((6,)),
        ],
        compiler_params=pltpu.CompilerParams(
            collective_id=0, has_side_effects=True, vmem_limit_bytes=48 << 20
        ),
    )(
        hidden_states,
        attn_gain.reshape(1, WIDTH),
        ffn_gain.reshape(1, WIDTH),
        w_query.reshape(HALF, HD),
        w_keyval.reshape(HALF, 32).T,
        w_out.reshape(HD, HALF),
        w_gate.T,
        w_up.T,
        w_down,
        kv_cache,
        lengths,
        first_shard,
    )


def solution(mesh):
    placed = (
        P(),
        P(),
        P(),
        P("grp", "rep", "tp", None),
        P("grp", "rep", "tp"),
        P("rep", "tp", None, "grp"),
        P("grp", ("tp", "rep")),
        P("grp", ("tp", "rep")),
        P(("tp", "rep"), "grp"),
        P(None, ("grp", "tp"), "rep", None),
        P(),
        P(),
    )
    return jax.shard_map(
        on_device,
        mesh=mesh,
        in_specs=placed,
        out_specs=P(None, ("grp", "tp", "rep")),
        check_vma=False,
    )
```

```python
import functools
import math

import numpy as np
import jax
import jax.numpy as jnp
from jax import lax
from jax.sharding import PartitionSpec as P
import jax.experimental.pallas as pl
import jax.experimental.pallas.tpu as pltpu

MESH = pl.DeviceIdType.MESH
NT = (((1,), (1,)), ((), ()))
epsilon = 1e-05
base_freq = 500000.0
masked = -1e30
floor_peak = -1e20

REQ = 8
WIDTH = 8192
HALF = WIDTH // 2
TILES = HALF // 128
HD = 128
CTX_DEV = 512
HEADS = 32
N_TP = 32
PEERS = 64
UNITS = 224
FREQ = [
    float(f)
    for f in (base_freq ** (-(2.0 * np.arange(HD // 2, dtype=np.float64)) / HD)).astype(np.float32)
]


def swap_halves(tile, diagonal):
    turned = pltpu.roll(pltpu.roll(tile, 64, 1), 4, 0)
    return jnp.where(diagonal, tile, turned)


def layer(
    hidden_ref, attn_gain_ref, ffn_gain_ref, wq_ref, wkv_ref, wo_ref, wg_ref, wu_ref, wd_ref,
    kv_ref, lengths_ref, first_shard_ref, out_ref,
    len_ref, first_ref, hid, gain_a, gain_f, wq, wkv, wo, wg, wu, wd, w_in, keys, keys_t, values,
    send_a, recv_a, q_rot, stage_c, send_c, recv_c, send_d, recv_d, recv_e, send_f, recv_f,
    send_g, recv_g, x_ffn, load_sem, kv_sem, send_sem, recv_sem,
):
    g = lax.axis_index("grp")
    t = lax.axis_index("tp")
    r = lax.axis_index("rep")
    me_row = g * N_TP + t
    me_col = t * 2 + r

    y, x, z = me_row // 16, (t // 4) % 4, t % 4

    def far_first(i):
        return 2 + i - (i // 2) * (2 * i - 1)

    def row_peer(k):
        there = (me_row + 1 + k) % PEERS
        return there, (there // N_TP, there % N_TP, r)

    def col_peer(k):
        there = (me_col + 1 + k) % PEERS
        return there, (g, there // 2, there % 2)

    barrier = pltpu.get_barrier_semaphore()

    @pl.loop(0, PEERS - 1)
    def _(k):
        _, dev = row_peer(k)
        pl.semaphore_signal(barrier, inc=1, device_id=dev, device_id_type=MESH)

    pl.semaphore_signal(barrier, inc=1, device_id=(g, t, 1 - r), device_id_type=MESH)

    own_half = pl.ds(pl.multiple_of(g * HALF, HALF), HALF)
    other_half = pl.ds(pl.multiple_of((1 - g) * HALF, HALF), HALF)
    loads = [
        (hidden_ref.at[:, own_half], hid.at[0]),
        (hidden_ref.at[:, other_half], hid.at[1]),
        (attn_gain_ref.at[:, own_half], gain_a),
        (wq_ref, wq),
        (wkv_ref, wkv),
        (ffn_gain_ref.at[:, own_half], gain_f),
        (wo_ref, wo),
        (wg_ref, wg),
        (wu_ref, wu),
        (wd_ref, wd),
        (lengths_ref, len_ref),
        (first_shard_ref, first_ref),
    ]
    copies = [pltpu.make_async_copy(s, d, load_sem.at[i]) for i, (s, d) in enumerate(loads)]
    kv_rows = kv_ref.reshape(REQ, 4 * CTX_DEV, 2 * HD)
    kv_copies = []
    for b in range(REQ):
        for i, dst in enumerate((keys, values)):
            kv_copies.append(
                pltpu.make_async_copy(
                    kv_rows.at[b, :, pl.ds(i * HD, HD)], dst.at[b], kv_sem.at[2 * b + i]
                )
            )
    for c in copies[:5] + copies[10:]:
        c.start()

    for c in copies[:5]:
        c.wait()
    for c in kv_copies[::2] + kv_copies[1::2] + copies[5:10]:
        c.start()
    own = hid[0].astype(jnp.float32)
    other = hid[1].astype(jnp.float32)
    squares = jnp.sum(own * own, axis=1, keepdims=True) + jnp.sum(
        other * other, axis=1, keepdims=True
    )
    scale = lax.rsqrt(squares * (1.0 / WIDTH) + epsilon)
    normed = (own * scale * gain_a[...]).astype(jnp.bfloat16)
    query_part = jnp.dot(normed, wq[...], preferred_element_type=jnp.float32)
    keyval_part = lax.dot_general(normed, wkv[...], NT, preferred_element_type=jnp.float32)
    keyval_wide = jnp.concatenate(
        (keyval_part, jnp.zeros((REQ, HD - 32), jnp.float32)), axis=1
    )
    spot = t % 4
    placed = keyval_wide
    for s in range(1, 4):
        placed = jnp.where(spot == s, pltpu.roll(keyval_wide, 32 * s, 1), placed)
    message = jnp.concatenate((query_part, placed), axis=0).astype(jnp.bfloat16)
    send_a[...] = message
    recv_a[me_row] = message

    pl.semaphore_wait(barrier, PEERS)

    def send_all(peer, source, landing, stage):
        @pl.loop(0, PEERS - 1)
        def _(k):
            p, dev = peer(k)
            pltpu.make_async_remote_copy(
                src_ref=source(p),
                dst_ref=landing,
                send_sem=send_sem.at[stage],
                recv_sem=recv_sem.at[stage],
                device_id=dev,
                device_id_type=MESH,
            ).start()

    def wait_all(buffer, sem):
        span = buffer.at[pl.ds(0, PEERS - 1)]
        pltpu.make_async_copy(span, span, sem).wait()

    send_all(row_peer, lambda p: send_a, recv_a.at[me_row], 0)

    lane8 = lax.broadcasted_iota(jnp.int32, (REQ, HD), 1)
    row8 = lax.broadcasted_iota(jnp.int32, (REQ, HD), 0)
    frequency = jnp.zeros((REQ, HD), jnp.float32)
    for i in range(HD // 2):
        frequency = jnp.where(lane8 // 2 == i, FREQ[i], frequency)
    position = jnp.zeros((REQ, HD), jnp.int32)
    for c in copies[10:]:
        c.wait()
    for b in range(REQ):
        position = jnp.where(row8 == b, len_ref[b], position)
    angles = position.astype(jnp.float32) * frequency
    cos_part = jnp.cos(angles)
    sin_part = jnp.sin(angles)
    even = lane8 % 2 == 0
    sin_even = jnp.where(even, -sin_part, 0.0)
    sin_odd = jnp.where(even, 0.0, sin_part)

    def rotate(x):
        return (
            x * cos_part + pltpu.roll(x, HD - 1, 1) * sin_even + pltpu.roll(x, 1, 1) * sin_odd
        )

    rounded = lambda x: x.astype(jnp.bfloat16).astype(jnp.float32)
    lane_row = lax.broadcasted_iota(jnp.int32, (REQ, 4 * CTX_DEV), 1)
    of_kv_head = [lane_row % 4 == i for i in range(4)]
    quarter = lane8 // 32
    diagonal = (lane8 < 64) == (row8 < 4)
    inv_scale = 1.0 / math.sqrt(HD)

    for b in range(REQ):
        kv_copies[2 * b].wait()
        keys_t[b] = keys[b].T

    wait_all(recv_a, recv_sem.at[0])
    for head in range(HEADS):
        pair = recv_a[head].astype(jnp.float32) + recv_a[N_TP + head].astype(jnp.float32)
        q_rot[pl.ds(head * REQ, REQ), :] = rounded(rotate(rounded(pair[:REQ])))

    def spread(row, op):
        for shift in (4, 8, 16, 32, 64):
            row = op(row, pltpu.roll(row, shift, 1))
        return row

    scores = []
    for b in range(REQ):
        q_b = q_rot[pl.ds(b, HEADS, stride=REQ), :].astype(jnp.bfloat16)
        scores.append(jnp.dot(q_b, keys_t[b], preferred_element_type=jnp.float32))
    weights = []
    for b in range(REQ):
        block = (me_row - first_ref[b]) & (PEERS - 1)
        live_rows = 4 * (len_ref[b] - block * CTX_DEV)
        grid = [scores[b][8 * i : 8 * i + 8] for i in range(4)]
        score = jnp.where(
            of_kv_head[0],
            grid[0],
            jnp.where(of_kv_head[1], grid[1], jnp.where(of_kv_head[2], grid[2], grid[3])),
        )
        score = jnp.where(lane_row < live_rows, score * inv_scale, masked)
        peak = functools.reduce(
            jnp.maximum, [score[:, HD * i : HD * i + HD] for i in range(4 * CTX_DEV // HD)]
        )
        peak = jnp.maximum(spread(peak, jnp.maximum), floor_peak)
        peak_hi = rounded(peak)
        peak_lo = rounded(peak - peak_hi)
        base = peak_hi + peak_lo
        weight = jnp.exp(score - jnp.concatenate([base] * (4 * CTX_DEV // HD), axis=1))
        total = functools.reduce(
            jnp.add, [weight[:, HD * i : HD * i + HD] for i in range(4 * CTX_DEV // HD)]
        )
        total = spread(total, jnp.add)
        total_hi = rounded(total)
        total_lo = rounded(total - total_hi)
        stats = jnp.where(
            quarter < 2,
            jnp.where(quarter == 0, peak_hi, peak_lo),
            jnp.where(quarter == 2, total_hi, total_lo),
        )
        for i in range(4):
            stage_c[pl.ds(REQ + b + 16 * 8 * i, 8, stride=16), :] = stats
        weights.append(
            jnp.concatenate(
                [jnp.where(of_kv_head[i], weight, 0.0) for i in range(4)], axis=0
            ).astype(jnp.bfloat16)
        )
    for b in range(REQ):
        kv_copies[2 * b + 1].wait()
    for b in range(REQ):
        stage_c[pl.ds(b, HEADS, stride=16), :] = jnp.dot(
            weights[b], values[b], preferred_element_type=jnp.float32
        )
    for head in range(HEADS):
        send_c[head] = stage_c[pl.ds(head * 16, 16), :].astype(jnp.bfloat16)
    recv_c[me_row] = send_c[t]
    send_all(row_peer, lambda p: send_c.at[p % N_TP], recv_c.at[me_row], 1)

    for c in copies[7:9]:
        c.wait()
    for first in (UNITS, 256 + UNITS):
        w_in[:, first : first + 256 - UNITS] = jnp.zeros((HALF, 256 - UNITS), jnp.bfloat16)
    w_in[:, :UNITS] = wg[...].T
    w_in[:, 256 : 256 + UNITS] = wu[...].T
    kv_first = (t // 8) * 8
    new_key = jnp.zeros((REQ, HD), jnp.float32)
    new_value = jnp.zeros((REQ, HD), jnp.float32)
    for j in range(4):
        part = recv_a[kv_first + j].astype(jnp.float32) + recv_a[N_TP + kv_first + j].astype(
            jnp.float32
        )
        new_key = new_key + part[REQ:]
        part = recv_a[kv_first + 4 + j].astype(jnp.float32) + recv_a[
            N_TP + kv_first + 4 + j
        ].astype(jnp.float32)
        new_value = new_value + part[REQ:]
    key_rot = rounded(rotate(rounded(new_key)))
    new_value = rounded(new_value)
    my_query = q_rot[pl.ds(pl.multiple_of(t * REQ, REQ), REQ), :]
    own_score = jnp.sum(my_query * key_rot, axis=1, keepdims=True) * inv_scale
    pick_row = lax.broadcasted_iota(jnp.int32, (HD, 2 * HD), 0)
    pick_col = lax.broadcasted_iota(jnp.int32, (HD, 2 * HD), 1)
    pick = jnp.where(
        (pick_row % 32 == t // 8) & (pick_row // 64 == pick_col // HD), 1.0, 0.0
    ).astype(jnp.bfloat16)

    wait_all(recv_c, recv_sem.at[1])
    partial = recv_c[...]
    stats_all = partial.astype(jnp.float32)[:, REQ:, :].reshape(PEERS * REQ, HD).astype(jnp.bfloat16)
    spread = jnp.dot(stats_all, pick, preferred_element_type=jnp.float32)
    peaks = spread[:, :HD].reshape(PEERS, REQ, HD)
    totals = spread[:, HD:].reshape(PEERS, REQ, HD)
    top = jnp.maximum(jnp.max(peaks, axis=0), own_score)
    keep = jnp.exp(peaks - top[None])
    own_weight = jnp.exp(own_score - top)
    numer = jnp.sum(keep * partial.astype(jnp.float32)[:, :REQ, :], axis=0)
    denom = jnp.sum(keep * totals, axis=0) + own_weight
    attended = ((numer + rounded(own_weight) * new_value) / denom).astype(jnp.bfloat16)

    def scatter(send, recv, row, weight, stage):
        for i in range(TILES // 2):
            product = jnp.dot(
                row, weight[:, pl.ds(i * 256, 256)], preferred_element_type=jnp.float32
            )
            for j in range(2):
                tile = swap_halves(product[:, j * 128 : j * 128 + 128], diagonal)
                send[4 * i + 2 * j] = tile[:4]
                send[4 * i + 2 * j + 1] = tile[4:]
        recv[me_col] = send[me_col]
        send_all(col_peer, lambda p: send.at[p], recv.at[me_col], stage)

    copies[6].wait()
    scatter(send_d, recv_d, attended, wo, 2)
    my_column = pl.ds(pl.multiple_of(t * 128, 128), 128)
    my_hidden = swap_halves(hid[0, :, my_column].astype(jnp.float32), diagonal)
    my_hidden = jnp.where(r == 0, my_hidden[:4], my_hidden[4:])
    wait_all(recv_d, recv_sem.at[2])
    projected = jnp.sum(recv_d[...], axis=0)
    recv_e[me_col] = projected
    send_all(col_peer, lambda p: recv_e.at[me_col], recv_e.at[me_col], 3)
    my_middle = rounded(my_hidden + projected)
    for c in copies[5:6] + copies[9:10]:
        c.wait()
    wait_all(recv_e, recv_sem.at[3])
    squares = jnp.zeros((REQ, HD), jnp.float32)
    for i in range(TILES):
        packed = jnp.concatenate((recv_e[2 * i], recv_e[2 * i + 1]), axis=0)
        col = pl.ds(i * 128, 128)
        middle = rounded(hid[0, :, col].astype(jnp.float32) + swap_halves(packed, diagonal))
        squares = squares + middle * middle
        x_ffn[:, col] = (middle * gain_f[:, col]).astype(jnp.bfloat16)

    product = jnp.dot(x_ffn[...], w_in[...], preferred_element_type=jnp.float32)
    gate_part = product[:, :UNITS]
    up_part = product[:, 256 : 256 + UNITS]
    square_sum = jnp.broadcast_to(jnp.sum(squares, axis=1, keepdims=True), (REQ, 256 - UNITS))
    send_f[0] = jnp.concatenate((gate_part, square_sum), axis=1)
    send_f[1] = jnp.concatenate((up_part, square_sum), axis=1)
    swap = pltpu.make_async_remote_copy(
        src_ref=send_f,
        dst_ref=recv_f,
        send_sem=send_sem.at[4],
        recv_sem=recv_sem.at[4],
        device_id=(1 - g, t, r),
        device_id_type=MESH,
    )
    swap.start()
    swap.wait_recv()
    gate_sum = send_f[0] + recv_f[0]
    up_sum = send_f[1] + recv_f[1]
    scale = lax.rsqrt(gate_sum[:, UNITS : UNITS + 1] * (1.0 / WIDTH) + epsilon)
    gate = gate_sum[:, :UNITS] * scale
    up = up_sum[:, :UNITS] * scale
    active = (gate / (1.0 + jnp.exp(-gate)) * up).astype(jnp.bfloat16)

    scatter(send_g, recv_g, active, wd, 5)
    wait_all(recv_g, recv_sem.at[5])
    result = my_middle + jnp.sum(recv_g[...], axis=0)
    out_ref[...] = jnp.concatenate((result[:, :64], result[:, 64:]), axis=0).astype(out_ref.dtype)

    wait_all(recv_a, send_sem.at[0])
    wait_all(recv_c, send_sem.at[1])
    wait_all(recv_d, send_sem.at[2])
    wait_all(recv_e, send_sem.at[3])
    swap.wait_send()
    wait_all(recv_g, send_sem.at[5])


def on_device(
    hidden_states, attn_gain, ffn_gain, w_query, w_keyval, w_out, w_gate, w_up, w_down,
    kv_cache, lengths, first_shard,
):
    outside = pl.BlockSpec(memory_space=pltpu.HBM)
    f32, bf16 = jnp.float32, jnp.bfloat16
    return pl.pallas_call(
        layer,
        out_shape=jax.ShapeDtypeStruct((REQ, 64), bf16),
        in_specs=[outside] * 12,
        out_specs=pl.BlockSpec(memory_space=pltpu.VMEM),
        scratch_shapes=[
            pltpu.SMEM((REQ,), jnp.int32),
            pltpu.SMEM((REQ,), jnp.int32),
            pltpu.VMEM((2, REQ, HALF), bf16),
            pltpu.VMEM((1, HALF), f32),
            pltpu.VMEM((1, HALF), f32),
            pltpu.VMEM((HALF, HD), bf16),
            pltpu.VMEM((32, HALF), bf16),
            pltpu.VMEM((HD, HALF), bf16),
            pltpu.VMEM((UNITS, HALF), bf16),
            pltpu.VMEM((UNITS, HALF), bf16),
            pltpu.VMEM((UNITS, HALF), bf16),
            pltpu.VMEM((HALF, 512), bf16),
            pltpu.VMEM((REQ, 4 * CTX_DEV, HD), bf16),
            pltpu.VMEM((REQ, HD, 4 * CTX_DEV), bf16),
            pltpu.VMEM((REQ, 4 * CTX_DEV, HD), bf16),
            pltpu.VMEM((16, HD), bf16),
            pltpu.VMEM((PEERS, 16, HD), bf16),
            pltpu.VMEM((HEADS * REQ, HD), f32),
            pltpu.VMEM((HEADS * 16, HD), f32),
            pltpu.VMEM((HEADS, 16, HD), bf16),
            pltpu.VMEM((PEERS, 16, HD), bf16),
            pltpu.VMEM((PEERS, 4, HD), f32),
            pltpu.VMEM((PEERS, 4, HD), f32),
            pltpu.VMEM((PEERS, 4, HD), f32),
            pltpu.VMEM((2, REQ, 256), f32),
            pltpu.VMEM((2, REQ, 256), f32),
            pltpu.VMEM((PEERS, 4, HD), f32),
            pltpu.VMEM((PEERS, 4, HD), f32),
            pltpu.VMEM((REQ, HALF), bf16),
            pltpu.SemaphoreType.DMA((12,)),
            pltpu.SemaphoreType.DMA((2 * REQ,)),
            pltpu.SemaphoreType.DMA((6,)),
            pltpu.SemaphoreType.DMA((6,)),
        ],
        compiler_params=pltpu.CompilerParams(
            collective_id=0, has_side_effects=True, vmem_limit_bytes=60 << 20
        ),
    )(
        hidden_states,
        attn_gain.reshape(1, WIDTH),
        ffn_gain.reshape(1, WIDTH),
        w_query.reshape(HALF, HD),
        w_keyval.reshape(HALF, 32).T,
        w_out.reshape(HD, HALF),
        w_gate.T,
        w_up.T,
        w_down,
        kv_cache,
        lengths,
        first_shard,
    )


def solution(mesh):
    placed = (
        P(),
        P(),
        P(),
        P("grp", "rep", "tp", None),
        P("grp", "rep", "tp"),
        P("rep", "tp", None, "grp"),
        P("grp", ("tp", "rep")),
        P("grp", ("tp", "rep")),
        P(("tp", "rep"), "grp"),
        P(None, ("grp", "tp"), "rep", None),
        P(),
        P(),
    )
    return jax.shard_map(
        on_device,
        mesh=mesh,
        in_specs=placed,
        out_specs=P(None, ("grp", "tp", "rep")),
        check_vma=False,
    )
```

```python
import functools
import math

import numpy as np
import jax
import jax.numpy as jnp
from jax import lax
from jax.sharding import PartitionSpec as P
import jax.experimental.pallas as pl
import jax.experimental.pallas.tpu as pltpu

MESH = pl.DeviceIdType.MESH
NT = (((1,), (1,)), ((), ()))
epsilon = 1e-05
base_freq = 500000.0
masked = -1e30
floor_peak = -1e20

REQ = 8
WIDTH = 8192
HALF = WIDTH // 2
TILES = HALF // 128
HD = 128
CTX_DEV = 512
HEADS = 32
N_TP = 32
PEERS = 64
KV_PEERS = 16
UNITS = 224
FREQ = [
    float(f)
    for f in (base_freq ** (-(2.0 * np.arange(HD // 2, dtype=np.float64)) / HD)).astype(np.float32)
]


def swap_halves(tile, diagonal):
    turned = pltpu.roll(pltpu.roll(tile, 64, 1), 4, 0)
    return jnp.where(diagonal, tile, turned)


def layer(
    hidden_ref, attn_gain_ref, ffn_gain_ref, wq_ref, wkv_ref, wo_ref, wg_ref, wu_ref, wd_ref,
    kv_ref, lengths_ref, first_shard_ref, out_ref,
    len_ref, first_ref, hid, gain_a, gain_f, wq, wkv, wo, wg, wu, wd, w_in, keys, keys_t, values,
    send_a, recv_a, recv_kv, q_rot, stage_c, send_c, recv_c, send_d, recv_d, recv_e, send_f, recv_f,
    send_g, recv_g, x_ffn, load_sem, kv_sem, send_sem, recv_sem,
):
    g = lax.axis_index("grp")
    t = lax.axis_index("tp")
    r = lax.axis_index("rep")
    me_row = g * N_TP + t
    me_col = t * 2 + r

    y, x, z = me_row // 16, (t // 4) % 4, t % 4

    def far_first(i):
        return 2 + i - (i // 2) * (2 * i - 1)

    def row_peer(k):
        there = (me_row + 1 + k) % PEERS
        return there, (there // N_TP, there % N_TP, r)

    me_kv = g * 8 + t % 8

    def kv_peer(k):
        there = (me_kv + 1 + k) % KV_PEERS
        return there, (there // 8, (t // 8) * 8 + there % 8, r)

    def col_peer(k):
        there = (me_col + 1 + k) % PEERS
        return there, (g, there // 2, there % 2)

    barrier = pltpu.get_barrier_semaphore()

    @pl.loop(0, PEERS - 1, unroll=True)
    def _(k):
        _, dev = row_peer(k)
        pl.semaphore_signal(barrier, inc=1, device_id=dev, device_id_type=MESH)

    pl.semaphore_signal(barrier, inc=1, device_id=(g, t, 1 - r), device_id_type=MESH)

    own_half = pl.ds(pl.multiple_of(g * HALF, HALF), HALF)
    other_half = pl.ds(pl.multiple_of((1 - g) * HALF, HALF), HALF)
    loads = [
        (hidden_ref.at[:, own_half], hid.at[0]),
        (hidden_ref.at[:, other_half], hid.at[1]),
        (attn_gain_ref.at[:, own_half], gain_a),
        (wq_ref, wq),
        (wkv_ref, wkv),
        (ffn_gain_ref.at[:, own_half], gain_f),
        (wo_ref, wo),
        (wg_ref, wg),
        (wu_ref, wu),
        (wd_ref, wd),
        (lengths_ref, len_ref),
        (first_shard_ref, first_ref),
    ]
    copies = [pltpu.make_async_copy(s, d, load_sem.at[i]) for i, (s, d) in enumerate(loads)]
    kv_rows = kv_ref.reshape(REQ, 4 * CTX_DEV, 2 * HD)
    kv_copies = []
    for b in range(REQ):
        for i, dst in enumerate((keys, values)):
            kv_copies.append(
                pltpu.make_async_copy(
                    kv_rows.at[b, :, pl.ds(i * HD, HD)], dst.at[b], kv_sem.at[2 * b + i]
                )
            )
    for c in copies[:5] + copies[10:]:
        c.start()

    for c in copies[:5]:
        c.wait()
    for c in kv_copies[::2] + kv_copies[1::2] + copies[5:10]:
        c.start()
    own = hid[0].astype(jnp.float32)
    other = hid[1].astype(jnp.float32)
    squares = jnp.sum(own * own, axis=1, keepdims=True) + jnp.sum(
        other * other, axis=1, keepdims=True
    )
    scale = lax.rsqrt(squares * (1.0 / WIDTH) + epsilon)
    normed = (own * scale * gain_a[...]).astype(jnp.bfloat16)
    query_part = jnp.dot(normed, wq[...], preferred_element_type=jnp.float32)
    keyval_part = lax.dot_general(normed, wkv[...], NT, preferred_element_type=jnp.float32)
    keyval_wide = jnp.concatenate(
        (keyval_part, jnp.zeros((REQ, HD - 32), jnp.float32)), axis=1
    )
    spot = t % 4
    placed = keyval_wide
    for s in range(1, 4):
        placed = jnp.where(spot == s, pltpu.roll(keyval_wide, 32 * s, 1), placed)
    send_a[0] = query_part.astype(jnp.bfloat16)
    recv_a[me_row] = send_a[0]
    send_a[1] = placed.astype(jnp.bfloat16)
    recv_kv[me_kv] = send_a[1]

    pl.semaphore_wait(barrier, PEERS)

    def send_all(peer, source, landing, stage, peers=PEERS):
        @pl.loop(0, peers - 1)
        def _(k):
            p, dev = peer(k)
            pltpu.make_async_remote_copy(
                src_ref=source(p),
                dst_ref=landing,
                send_sem=send_sem.at[stage],
                recv_sem=recv_sem.at[stage],
                device_id=dev,
                device_id_type=MESH,
            ).start()

    def wait_all(buffer, sem, peers=PEERS):
        span = buffer.at[pl.ds(0, peers - 1)]
        pltpu.make_async_copy(span, span, sem).wait()

    send_all(row_peer, lambda p: send_a.at[0], recv_a.at[me_row], 0)
    send_all(kv_peer, lambda p: send_a.at[1], recv_kv.at[me_kv], 6, KV_PEERS)

    lane8 = lax.broadcasted_iota(jnp.int32, (REQ, HD), 1)
    row8 = lax.broadcasted_iota(jnp.int32, (REQ, HD), 0)
    frequency = jnp.zeros((REQ, HD), jnp.float32)
    for i in range(HD // 2):
        frequency = jnp.where(lane8 // 2 == i, FREQ[i], frequency)
    position = jnp.zeros((REQ, HD), jnp.int32)
    for c in copies[10:]:
        c.wait()
    for b in range(REQ):
        position = jnp.where(row8 == b, len_ref[b], position)
    angles = position.astype(jnp.float32) * frequency
    cos_part = jnp.cos(angles)
    sin_part = jnp.sin(angles)
    even = lane8 % 2 == 0
    sin_even = jnp.where(even, -sin_part, 0.0)
    sin_odd = jnp.where(even, 0.0, sin_part)

    def rotate(x):
        return (
            x * cos_part + pltpu.roll(x, HD - 1, 1) * sin_even + pltpu.roll(x, 1, 1) * sin_odd
        )

    rounded = lambda x: x.astype(jnp.bfloat16).astype(jnp.float32)
    lane_row = lax.broadcasted_iota(jnp.int32, (REQ, 4 * CTX_DEV), 1)
    of_kv_head = [lane_row % 4 == i for i in range(4)]
    quarter = lane8 // 32
    diagonal = (lane8 < 64) == (row8 < 4)
    inv_scale = 1.0 / math.sqrt(HD)

    for b in range(REQ):
        kv_copies[2 * b].wait()
        keys_t[b] = keys[b].T

    wait_all(recv_a, recv_sem.at[0])
    for head in range(HEADS):
        pair = recv_a[head].astype(jnp.float32) + recv_a[N_TP + head].astype(jnp.float32)
        q_rot[pl.ds(head * REQ, REQ), :] = rounded(rotate(rounded(pair)))

    def spread(row, op):
        for shift in (4, 8, 16, 32, 64):
            row = op(row, pltpu.roll(row, shift, 1))
        return row

    scores = []
    for b in range(REQ):
        q_b = q_rot[pl.ds(b, HEADS, stride=REQ), :].astype(jnp.bfloat16)
        scores.append(jnp.dot(q_b, keys_t[b], preferred_element_type=jnp.float32))
    weights = []
    for b in range(REQ):
        block = (me_row - first_ref[b]) & (PEERS - 1)
        live_rows = 4 * (len_ref[b] - block * CTX_DEV)
        grid = [scores[b][8 * i : 8 * i + 8] for i in range(4)]
        score = jnp.where(
            of_kv_head[0],
            grid[0],
            jnp.where(of_kv_head[1], grid[1], jnp.where(of_kv_head[2], grid[2], grid[3])),
        )
        score = jnp.where(lane_row < live_rows, score * inv_scale, masked)
        peak = functools.reduce(
            jnp.maximum, [score[:, HD * i : HD * i + HD] for i in range(4 * CTX_DEV // HD)]
        )
        peak = jnp.maximum(spread(peak, jnp.maximum), floor_peak)
        peak_hi = rounded(peak)
        peak_lo = rounded(peak - peak_hi)
        base = peak_hi + peak_lo
        weight = jnp.exp(score - jnp.concatenate([base] * (4 * CTX_DEV // HD), axis=1))
        total = functools.reduce(
            jnp.add, [weight[:, HD * i : HD * i + HD] for i in range(4 * CTX_DEV // HD)]
        )
        total = spread(total, jnp.add)
        total_hi = rounded(total)
        total_lo = rounded(total - total_hi)
        stats = jnp.where(
            quarter < 2,
            jnp.where(quarter == 0, peak_hi, peak_lo),
            jnp.where(quarter == 2, total_hi, total_lo),
        )
        for i in range(4):
            stage_c[pl.ds(REQ + b + 16 * 8 * i, 8, stride=16), :] = stats
        weights.append(
            jnp.concatenate(
                [jnp.where(of_kv_head[i], weight, 0.0) for i in range(4)], axis=0
            ).astype(jnp.bfloat16)
        )
    for b in range(REQ):
        kv_copies[2 * b + 1].wait()
    for b in range(REQ):
        stage_c[pl.ds(b, HEADS, stride=16), :] = jnp.dot(
            weights[b], values[b], preferred_element_type=jnp.float32
        )
    for head in range(HEADS):
        send_c[head] = stage_c[pl.ds(head * 16, 16), :].astype(jnp.bfloat16)
    recv_c[me_row] = send_c[t]
    send_all(row_peer, lambda p: send_c.at[p % N_TP], recv_c.at[me_row], 1)

    for c in copies[7:9]:
        c.wait()
    for first in (UNITS, 256 + UNITS):
        w_in[:, first : first + 256 - UNITS] = jnp.zeros((HALF, 256 - UNITS), jnp.bfloat16)
    w_in[:, :UNITS] = wg[...].T
    w_in[:, 256 : 256 + UNITS] = wu[...].T
    wait_all(recv_kv, recv_sem.at[6], KV_PEERS)
    new_key = jnp.zeros((REQ, HD), jnp.float32)
    new_value = jnp.zeros((REQ, HD), jnp.float32)
    for j in range(4):
        new_key = new_key + (recv_kv[j].astype(jnp.float32) + recv_kv[8 + j].astype(jnp.float32))
        new_value = new_value + (
            recv_kv[4 + j].astype(jnp.float32) + recv_kv[12 + j].astype(jnp.float32)
        )
    key_rot = rounded(rotate(rounded(new_key)))
    new_value = rounded(new_value)
    my_query = q_rot[pl.ds(pl.multiple_of(t * REQ, REQ), REQ), :]
    own_score = jnp.sum(my_query * key_rot, axis=1, keepdims=True) * inv_scale
    pick_row = lax.broadcasted_iota(jnp.int32, (HD, 2 * HD), 0)
    pick_col = lax.broadcasted_iota(jnp.int32, (HD, 2 * HD), 1)
    pick = jnp.where(
        (pick_row % 32 == t // 8) & (pick_row // 64 == pick_col // HD), 1.0, 0.0
    ).astype(jnp.bfloat16)

    wait_all(recv_c, recv_sem.at[1])
    partial = recv_c[...]
    stats_all = partial.astype(jnp.float32)[:, REQ:, :].reshape(PEERS * REQ, HD).astype(jnp.bfloat16)
    spread = jnp.dot(stats_all, pick, preferred_element_type=jnp.float32)
    peaks = spread[:, :HD].reshape(PEERS, REQ, HD)
    totals = spread[:, HD:].reshape(PEERS, REQ, HD)
    top = jnp.maximum(jnp.max(peaks, axis=0), own_score)
    keep = jnp.exp(peaks - top[None])
    own_weight = jnp.exp(own_score - top)
    numer = jnp.sum(keep * partial.astype(jnp.float32)[:, :REQ, :], axis=0)
    denom = jnp.sum(keep * totals, axis=0) + own_weight
    attended = ((numer + rounded(own_weight) * new_value) / denom).astype(jnp.bfloat16)

    def scatter(send, recv, row, weight, stage):
        for i in range(TILES // 2):
            product = jnp.dot(
                row, weight[:, pl.ds(i * 256, 256)], preferred_element_type=jnp.float32
            )
            for j in range(2):
                tile = swap_halves(product[:, j * 128 : j * 128 + 128], diagonal)
                send[4 * i + 2 * j] = tile[:4]
                send[4 * i + 2 * j + 1] = tile[4:]
        recv[me_col] = send[me_col]
        send_all(col_peer, lambda p: send.at[p], recv.at[me_col], stage)

    copies[6].wait()
    scatter(send_d, recv_d, attended, wo, 2)
    my_column = pl.ds(pl.multiple_of(t * 128, 128), 128)
    my_hidden = swap_halves(hid[0, :, my_column].astype(jnp.float32), diagonal)
    my_hidden = jnp.where(r == 0, my_hidden[:4], my_hidden[4:])
    wait_all(recv_d, recv_sem.at[2])
    projected = jnp.sum(recv_d[...], axis=0)
    recv_e[me_col] = projected
    send_all(col_peer, lambda p: recv_e.at[me_col], recv_e.at[me_col], 3)
    my_middle = rounded(my_hidden + projected)
    for c in copies[5:6] + copies[9:10]:
        c.wait()
    wait_all(recv_e, recv_sem.at[3])
    squares = jnp.zeros((REQ, HD), jnp.float32)
    for i in range(TILES):
        packed = jnp.concatenate((recv_e[2 * i], recv_e[2 * i + 1]), axis=0)
        col = pl.ds(i * 128, 128)
        middle = rounded(hid[0, :, col].astype(jnp.float32) + swap_halves(packed, diagonal))
        squares = squares + middle * middle
        x_ffn[:, col] = (middle * gain_f[:, col]).astype(jnp.bfloat16)

    product = jnp.dot(x_ffn[...], w_in[...], preferred_element_type=jnp.float32)
    gate_part = product[:, :UNITS]
    up_part = product[:, 256 : 256 + UNITS]
    square_sum = jnp.broadcast_to(jnp.sum(squares, axis=1, keepdims=True), (REQ, 256 - UNITS))
    send_f[0] = jnp.concatenate((gate_part, square_sum), axis=1)
    send_f[1] = jnp.concatenate((up_part, square_sum), axis=1)
    swap = pltpu.make_async_remote_copy(
        src_ref=send_f,
        dst_ref=recv_f,
        send_sem=send_sem.at[4],
        recv_sem=recv_sem.at[4],
        device_id=(1 - g, t, r),
        device_id_type=MESH,
    )
    swap.start()
    swap.wait_recv()
    gate_sum = send_f[0] + recv_f[0]
    up_sum = send_f[1] + recv_f[1]
    scale = lax.rsqrt(gate_sum[:, UNITS : UNITS + 1] * (1.0 / WIDTH) + epsilon)
    gate = gate_sum[:, :UNITS] * scale
    up = up_sum[:, :UNITS] * scale
    active = (gate / (1.0 + jnp.exp(-gate)) * up).astype(jnp.bfloat16)

    scatter(send_g, recv_g, active, wd, 5)
    wait_all(recv_g, recv_sem.at[5])
    result = my_middle + jnp.sum(recv_g[...], axis=0)
    out_ref[...] = jnp.concatenate((result[:, :64], result[:, 64:]), axis=0).astype(out_ref.dtype)

    wait_all(recv_a, send_sem.at[0])
    wait_all(recv_kv, send_sem.at[6], KV_PEERS)
    wait_all(recv_c, send_sem.at[1])
    wait_all(recv_d, send_sem.at[2])
    wait_all(recv_e, send_sem.at[3])
    swap.wait_send()
    wait_all(recv_g, send_sem.at[5])


def on_device(
    hidden_states, attn_gain, ffn_gain, w_query, w_keyval, w_out, w_gate, w_up, w_down,
    kv_cache, lengths, first_shard,
):
    outside = pl.BlockSpec(memory_space=pltpu.HBM)
    f32, bf16 = jnp.float32, jnp.bfloat16
    return pl.pallas_call(
        layer,
        out_shape=jax.ShapeDtypeStruct((REQ, 64), bf16),
        in_specs=[outside] * 12,
        out_specs=pl.BlockSpec(memory_space=pltpu.VMEM),
        scratch_shapes=[
            pltpu.SMEM((REQ,), jnp.int32),
            pltpu.SMEM((REQ,), jnp.int32),
            pltpu.VMEM((2, REQ, HALF), bf16),
            pltpu.VMEM((1, HALF), f32),
            pltpu.VMEM((1, HALF), f32),
            pltpu.VMEM((HALF, HD), bf16),
            pltpu.VMEM((32, HALF), bf16),
            pltpu.VMEM((HD, HALF), bf16),
            pltpu.VMEM((UNITS, HALF), bf16),
            pltpu.VMEM((UNITS, HALF), bf16),
            pltpu.VMEM((UNITS, HALF), bf16),
            pltpu.VMEM((HALF, 512), bf16),
            pltpu.VMEM((REQ, 4 * CTX_DEV, HD), bf16),
            pltpu.VMEM((REQ, HD, 4 * CTX_DEV), bf16),
            pltpu.VMEM((REQ, 4 * CTX_DEV, HD), bf16),
            pltpu.VMEM((2, REQ, HD), bf16),
            pltpu.VMEM((PEERS, REQ, HD), bf16),
            pltpu.VMEM((KV_PEERS, REQ, HD), bf16),
            pltpu.VMEM((HEADS * REQ, HD), f32),
            pltpu.VMEM((HEADS * 16, HD), f32),
            pltpu.VMEM((HEADS, 16, HD), bf16),
            pltpu.VMEM((PEERS, 16, HD), bf16),
            pltpu.VMEM((PEERS, 4, HD), f32),
            pltpu.VMEM((PEERS, 4, HD), f32),
            pltpu.VMEM((PEERS, 4, HD), f32),
            pltpu.VMEM((2, REQ, 256), f32),
            pltpu.VMEM((2, REQ, 256), f32),
            pltpu.VMEM((PEERS, 4, HD), f32),
            pltpu.VMEM((PEERS, 4, HD), f32),
            pltpu.VMEM((REQ, HALF), bf16),
            pltpu.SemaphoreType.DMA((12,)),
            pltpu.SemaphoreType.DMA((2 * REQ,)),
            pltpu.SemaphoreType.DMA((7,)),
            pltpu.SemaphoreType.DMA((7,)),
        ],
        compiler_params=pltpu.CompilerParams(
            collective_id=0, has_side_effects=True, vmem_limit_bytes=60 << 20
        ),
    )(
        hidden_states,
        attn_gain.reshape(1, WIDTH),
        ffn_gain.reshape(1, WIDTH),
        w_query.reshape(HALF, HD),
        w_keyval.reshape(HALF, 32).T,
        w_out.reshape(HD, HALF),
        w_gate.T,
        w_up.T,
        w_down,
        kv_cache,
        lengths,
        first_shard,
    )


def solution(mesh):
    placed = (
        P(),
        P(),
        P(),
        P("grp", "rep", "tp", None),
        P("grp", "rep", "tp"),
        P("rep", "tp", None, "grp"),
        P("grp", ("tp", "rep")),
        P("grp", ("tp", "rep")),
        P(("tp", "rep"), "grp"),
        P(None, ("grp", "tp"), "rep", None),
        P(),
        P(),
    )
    return jax.shard_map(
        on_device,
        mesh=mesh,
        in_specs=placed,
        out_specs=P(None, ("grp", "tp", "rep")),
        check_vma=False,
    )
```

```python
import functools
import math

import numpy as np
import jax
import jax.numpy as jnp
from jax import lax
from jax.sharding import PartitionSpec as P
import jax.experimental.pallas as pl
import jax.experimental.pallas.tpu as pltpu

MESH = pl.DeviceIdType.MESH
NT = (((1,), (1,)), ((), ()))
epsilon = 1e-05
base_freq = 500000.0
masked = -1e30
floor_peak = -1e20

REQ = 8
WIDTH = 8192
HALF = WIDTH // 2
TILES = HALF // 128
HD = 128
CTX_DEV = 512
HEADS = 32
N_TP = 32
PEERS = 64
KV_PEERS = 16
UNITS = 224
FREQ = [
    float(f)
    for f in (base_freq ** (-(2.0 * np.arange(HD // 2, dtype=np.float64)) / HD)).astype(np.float32)
]


def swap_halves(tile, diagonal):
    turned = pltpu.roll(pltpu.roll(tile, 64, 1), 4, 0)
    return jnp.where(diagonal, tile, turned)


def layer(
    hidden_ref, attn_gain_ref, ffn_gain_ref, wq_ref, wkv_ref, wo_ref, wg_ref, wu_ref, wd_ref,
    kv_ref, lengths_ref, first_shard_ref, out_ref,
    len_ref, first_ref, hid, gain_a, gain_f, wq, wkv, wo, wg, wu, wd, w_in, keys, keys_t, values,
    send_a, recv_a, recv_kv, q_rot, stage_c, send_c, recv_c, send_d, recv_d, recv_e, send_f, recv_f,
    send_g, recv_g, x_ffn, load_sem, kv_sem, send_sem, recv_sem,
):
    g = lax.axis_index("grp")
    t = lax.axis_index("tp")
    r = lax.axis_index("rep")
    me_row = g * N_TP + t
    me_col = t * 2 + r

    y, x, z = me_row // 16, (t // 4) % 4, t % 4

    def far_first(i):
        return 2 + i - (i // 2) * (2 * i - 1)

    def row_peer(k):
        there = lax.rem(me_row + 1 + k, PEERS)
        return there, (lax.div(there, N_TP), lax.rem(there, N_TP), r)

    kv_first = (t // 8) * 8
    me_kv = g * 8 + t % 8

    def kv_peer(k):
        there = lax.rem(me_kv + 1 + k, KV_PEERS)
        return there, (lax.div(there, 8), kv_first + lax.rem(there, 8), r)

    def col_peer(k):
        there = lax.rem(me_col + 1 + k, PEERS)
        return there, (g, lax.div(there, 2), lax.rem(there, 2))

    barrier = pltpu.get_barrier_semaphore()

    @pl.loop(0, PEERS - 1, unroll=True)
    def _(k):
        _, dev = row_peer(k)
        pl.semaphore_signal(barrier, inc=1, device_id=dev, device_id_type=MESH)

    pl.semaphore_signal(barrier, inc=1, device_id=(g, t, 1 - r), device_id_type=MESH)

    own_half = pl.ds(pl.multiple_of(g * HALF, HALF), HALF)
    other_half = pl.ds(pl.multiple_of((1 - g) * HALF, HALF), HALF)
    loads = [
        (hidden_ref.at[:, own_half], hid.at[0]),
        (hidden_ref.at[:, other_half], hid.at[1]),
        (attn_gain_ref.at[:, own_half], gain_a),
        (wq_ref, wq),
        (wkv_ref, wkv),
        (ffn_gain_ref.at[:, own_half], gain_f),
        (wo_ref, wo),
        (wg_ref, wg),
        (wu_ref, wu),
        (wd_ref, wd),
        (lengths_ref, len_ref),
        (first_shard_ref, first_ref),
    ]
    copies = [pltpu.make_async_copy(s, d, load_sem.at[i]) for i, (s, d) in enumerate(loads)]
    kv_rows = kv_ref.reshape(REQ, 4 * CTX_DEV, 2 * HD)
    kv_copies = []
    for b in range(REQ):
        for i, dst in enumerate((keys, values)):
            kv_copies.append(
                pltpu.make_async_copy(
                    kv_rows.at[b, :, pl.ds(i * HD, HD)], dst.at[b], kv_sem.at[2 * b + i]
                )
            )
    for c in copies[:5] + copies[10:]:
        c.start()

    for c in copies[:5]:
        c.wait()
    for c in kv_copies[::2] + kv_copies[1::2] + copies[5:10]:
        c.start()
    own = hid[0].astype(jnp.float32)
    other = hid[1].astype(jnp.float32)
    squares = jnp.sum(own * own, axis=1, keepdims=True) + jnp.sum(
        other * other, axis=1, keepdims=True
    )
    scale = lax.rsqrt(squares * (1.0 / WIDTH) + epsilon)
    normed = (own * scale * gain_a[...]).astype(jnp.bfloat16)
    query_part = jnp.dot(normed, wq[...], preferred_element_type=jnp.float32)
    keyval_part = lax.dot_general(normed, wkv[...], NT, preferred_element_type=jnp.float32)
    keyval_wide = jnp.concatenate(
        (keyval_part, jnp.zeros((REQ, HD - 32), jnp.float32)), axis=1
    )
    spot = t % 4
    placed = keyval_wide
    for s in range(1, 4):
        placed = jnp.where(spot == s, pltpu.roll(keyval_wide, 32 * s, 1), placed)
    send_a[0] = query_part.astype(jnp.bfloat16)
    recv_a[me_row] = send_a[0]
    send_a[1] = placed.astype(jnp.bfloat16)
    recv_kv[me_kv] = send_a[1]

    pl.semaphore_wait(barrier, PEERS)

    def send_all(peer, source, landing, stage, peers=PEERS):
        @pl.loop(0, peers - 1, unroll=9 if peers == PEERS else 1)
        def _(k):
            p, dev = peer(k)
            pltpu.make_async_remote_copy(
                src_ref=source(p),
                dst_ref=landing,
                send_sem=send_sem.at[stage],
                recv_sem=recv_sem.at[stage],
                device_id=dev,
                device_id_type=MESH,
            ).start()

    def wait_all(buffer, sem, peers=PEERS):
        span = buffer.at[pl.ds(0, peers - 1)]
        pltpu.make_async_copy(span, span, sem).wait()

    send_all(row_peer, lambda p: send_a.at[0], recv_a.at[me_row], 0)
    send_all(kv_peer, lambda p: send_a.at[1], recv_kv.at[me_kv], 6, KV_PEERS)

    lane8 = lax.broadcasted_iota(jnp.int32, (REQ, HD), 1)
    row8 = lax.broadcasted_iota(jnp.int32, (REQ, HD), 0)
    frequency = jnp.zeros((REQ, HD), jnp.float32)
    for i in range(HD // 2):
        frequency = jnp.where(lane8 // 2 == i, FREQ[i], frequency)
    position = jnp.zeros((REQ, HD), jnp.int32)
    for c in copies[10:]:
        c.wait()
    for b in range(REQ):
        position = jnp.where(row8 == b, len_ref[b], position)
    angles = position.astype(jnp.float32) * frequency
    cos_part = jnp.cos(angles)
    sin_part = jnp.sin(angles)
    even = lane8 % 2 == 0
    sin_even = jnp.where(even, -sin_part, 0.0)
    sin_odd = jnp.where(even, 0.0, sin_part)

    def rotate(x):
        return (
            x * cos_part + pltpu.roll(x, HD - 1, 1) * sin_even + pltpu.roll(x, 1, 1) * sin_odd
        )

    rounded = lambda x: x.astype(jnp.bfloat16).astype(jnp.float32)
    lane_row = lax.broadcasted_iota(jnp.int32, (REQ, 4 * CTX_DEV), 1)
    of_kv_head = [lane_row % 4 == i for i in range(4)]
    quarter = lane8 // 32
    diagonal = (lane8 < 64) == (row8 < 4)
    inv_scale = 1.0 / math.sqrt(HD)

    for b in range(REQ):
        kv_copies[2 * b].wait()
        keys_t[b] = keys[b].T

    wait_all(recv_a, recv_sem.at[0])
    for head in range(HEADS):
        pair = recv_a[head].astype(jnp.float32) + recv_a[N_TP + head].astype(jnp.float32)
        q_rot[pl.ds(head * REQ, REQ), :] = rounded(rotate(rounded(pair)))

    def spread(row, op):
        for shift in (4, 8, 16, 32, 64):
            row = op(row, pltpu.roll(row, shift, 1))
        return row

    scores = []
    for b in range(REQ):
        q_b = q_rot[pl.ds(b, HEADS, stride=REQ), :].astype(jnp.bfloat16)
        scores.append(jnp.dot(q_b, keys_t[b], preferred_element_type=jnp.float32))
    weights = []
    for b in range(REQ):
        block = (me_row - first_ref[b]) & (PEERS - 1)
        live_rows = 4 * (len_ref[b] - block * CTX_DEV)
        grid = [scores[b][8 * i : 8 * i + 8] for i in range(4)]
        score = jnp.where(
            of_kv_head[0],
            grid[0],
            jnp.where(of_kv_head[1], grid[1], jnp.where(of_kv_head[2], grid[2], grid[3])),
        )
        score = jnp.where(lane_row < live_rows, score * inv_scale, masked)
        peak = functools.reduce(
            jnp.maximum, [score[:, HD * i : HD * i + HD] for i in range(4 * CTX_DEV // HD)]
        )
        peak = jnp.maximum(spread(peak, jnp.maximum), floor_peak)
        peak_hi = rounded(peak)
        peak_lo = rounded(peak - peak_hi)
        base = peak_hi + peak_lo
        weight = jnp.exp(score - jnp.concatenate([base] * (4 * CTX_DEV // HD), axis=1))
        total = functools.reduce(
            jnp.add, [weight[:, HD * i : HD * i + HD] for i in range(4 * CTX_DEV // HD)]
        )
        total = spread(total, jnp.add)
        total_hi = rounded(total)
        total_lo = rounded(total - total_hi)
        stats = jnp.where(
            quarter < 2,
            jnp.where(quarter == 0, peak_hi, peak_lo),
            jnp.where(quarter == 2, total_hi, total_lo),
        )
        for i in range(4):
            stage_c[pl.ds(REQ + b + 16 * 8 * i, 8, stride=16), :] = stats
        weights.append(
            jnp.concatenate(
                [jnp.where(of_kv_head[i], weight, 0.0) for i in range(4)], axis=0
            ).astype(jnp.bfloat16)
        )
    for b in range(REQ):
        kv_copies[2 * b + 1].wait()
    for b in range(REQ):
        stage_c[pl.ds(b, HEADS, stride=16), :] = jnp.dot(
            weights[b], values[b], preferred_element_type=jnp.float32
        )
    for head in range(HEADS):
        send_c[head] = stage_c[pl.ds(head * 16, 16), :].astype(jnp.bfloat16)
    recv_c[me_row] = send_c[t]
    send_all(row_peer, lambda p: send_c.at[lax.rem(p, N_TP)], recv_c.at[me_row], 1)

    for c in copies[7:9]:
        c.wait()
    for first in (UNITS, 256 + UNITS):
        w_in[:, first : first + 256 - UNITS] = jnp.zeros((HALF, 256 - UNITS), jnp.bfloat16)
    w_in[:, :UNITS] = wg[...].T
    w_in[:, 256 : 256 + UNITS] = wu[...].T
    wait_all(recv_kv, recv_sem.at[6], KV_PEERS)
    new_key = jnp.zeros((REQ, HD), jnp.float32)
    new_value = jnp.zeros((REQ, HD), jnp.float32)
    for j in range(4):
        new_key = new_key + (recv_kv[j].astype(jnp.float32) + recv_kv[8 + j].astype(jnp.float32))
        new_value = new_value + (
            recv_kv[4 + j].astype(jnp.float32) + recv_kv[12 + j].astype(jnp.float32)
        )
    key_rot = rounded(rotate(rounded(new_key)))
    new_value = rounded(new_value)
    my_query = q_rot[pl.ds(pl.multiple_of(t * REQ, REQ), REQ), :]
    own_score = jnp.sum(my_query * key_rot, axis=1, keepdims=True) * inv_scale
    pick_row = lax.broadcasted_iota(jnp.int32, (HD, 2 * HD), 0)
    pick_col = lax.broadcasted_iota(jnp.int32, (HD, 2 * HD), 1)
    pick = jnp.where(
        (pick_row % 32 == t // 8) & (pick_row // 64 == pick_col // HD), 1.0, 0.0
    ).astype(jnp.bfloat16)

    wait_all(recv_c, recv_sem.at[1])
    partial = recv_c[...]
    stats_all = partial.astype(jnp.float32)[:, REQ:, :].reshape(PEERS * REQ, HD).astype(jnp.bfloat16)
    spread = jnp.dot(stats_all, pick, preferred_element_type=jnp.float32)
    peaks = spread[:, :HD].reshape(PEERS, REQ, HD)
    totals = spread[:, HD:].reshape(PEERS, REQ, HD)
    top = jnp.maximum(jnp.max(peaks, axis=0), own_score)
    keep = jnp.exp(peaks - top[None])
    own_weight = jnp.exp(own_score - top)
    numer = jnp.sum(keep * partial.astype(jnp.float32)[:, :REQ, :], axis=0)
    denom = jnp.sum(keep * totals, axis=0) + own_weight
    attended = ((numer + rounded(own_weight) * new_value) / denom).astype(jnp.bfloat16)

    def scatter(send, recv, row, weight, stage):
        for i in range(TILES // 2):
            product = jnp.dot(
                row, weight[:, pl.ds(i * 256, 256)], preferred_element_type=jnp.float32
            )
            for j in range(2):
                tile = swap_halves(product[:, j * 128 : j * 128 + 128], diagonal)
                send[4 * i + 2 * j] = tile[:4]
                send[4 * i + 2 * j + 1] = tile[4:]
        recv[me_col] = send[me_col]
        send_all(col_peer, lambda p: send.at[p], recv.at[me_col], stage)

    copies[6].wait()
    scatter(send_d, recv_d, attended, wo, 2)
    my_column = pl.ds(pl.multiple_of(t * 128, 128), 128)
    my_hidden = swap_halves(hid[0, :, my_column].astype(jnp.float32), diagonal)
    my_hidden = jnp.where(r == 0, my_hidden[:4], my_hidden[4:])
    wait_all(recv_d, recv_sem.at[2])
    projected = jnp.sum(recv_d[...], axis=0)
    recv_e[me_col] = projected
    send_all(col_peer, lambda p: recv_e.at[me_col], recv_e.at[me_col], 3)
    my_middle = rounded(my_hidden + projected)
    for c in copies[5:6] + copies[9:10]:
        c.wait()
    wait_all(recv_e, recv_sem.at[3])
    squares = jnp.zeros((REQ, HD), jnp.float32)
    for i in range(TILES):
        packed = jnp.concatenate((recv_e[2 * i], recv_e[2 * i + 1]), axis=0)
        col = pl.ds(i * 128, 128)
        middle = rounded(hid[0, :, col].astype(jnp.float32) + swap_halves(packed, diagonal))
        squares = squares + middle * middle
        x_ffn[:, col] = (middle * gain_f[:, col]).astype(jnp.bfloat16)

    product = jnp.dot(x_ffn[...], w_in[...], preferred_element_type=jnp.float32)
    gate_part = product[:, :UNITS]
    up_part = product[:, 256 : 256 + UNITS]
    square_sum = jnp.broadcast_to(jnp.sum(squares, axis=1, keepdims=True), (REQ, 256 - UNITS))
    send_f[0] = jnp.concatenate((gate_part, square_sum), axis=1)
    send_f[1] = jnp.concatenate((up_part, square_sum), axis=1)
    swap = pltpu.make_async_remote_copy(
        src_ref=send_f,
        dst_ref=recv_f,
        send_sem=send_sem.at[4],
        recv_sem=recv_sem.at[4],
        device_id=(1 - g, t, r),
        device_id_type=MESH,
    )
    swap.start()
    swap.wait_recv()
    gate_sum = send_f[0] + recv_f[0]
    up_sum = send_f[1] + recv_f[1]
    scale = lax.rsqrt(gate_sum[:, UNITS : UNITS + 1] * (1.0 / WIDTH) + epsilon)
    gate = gate_sum[:, :UNITS] * scale
    up = up_sum[:, :UNITS] * scale
    active = (gate / (1.0 + jnp.exp(-gate)) * up).astype(jnp.bfloat16)

    scatter(send_g, recv_g, active, wd, 5)
    wait_all(recv_g, recv_sem.at[5])
    result = my_middle + jnp.sum(recv_g[...], axis=0)
    out_ref[...] = jnp.concatenate((result[:, :64], result[:, 64:]), axis=0).astype(out_ref.dtype)

    wait_all(recv_a, send_sem.at[0])
    wait_all(recv_kv, send_sem.at[6], KV_PEERS)
    wait_all(recv_c, send_sem.at[1])
    wait_all(recv_d, send_sem.at[2])
    wait_all(recv_e, send_sem.at[3])
    swap.wait_send()
    wait_all(recv_g, send_sem.at[5])


def on_device(
    hidden_states, attn_gain, ffn_gain, w_query, w_keyval, w_out, w_gate, w_up, w_down,
    kv_cache, lengths, first_shard,
):
    outside = pl.BlockSpec(memory_space=pltpu.HBM)
    f32, bf16 = jnp.float32, jnp.bfloat16
    return pl.pallas_call(
        layer,
        out_shape=jax.ShapeDtypeStruct((REQ, 64), bf16),
        in_specs=[outside] * 12,
        out_specs=pl.BlockSpec(memory_space=pltpu.VMEM),
        scratch_shapes=[
            pltpu.SMEM((REQ,), jnp.int32),
            pltpu.SMEM((REQ,), jnp.int32),
            pltpu.VMEM((2, REQ, HALF), bf16),
            pltpu.VMEM((1, HALF), f32),
            pltpu.VMEM((1, HALF), f32),
            pltpu.VMEM((HALF, HD), bf16),
            pltpu.VMEM((32, HALF), bf16),
            pltpu.VMEM((HD, HALF), bf16),
            pltpu.VMEM((UNITS, HALF), bf16),
            pltpu.VMEM((UNITS, HALF), bf16),
            pltpu.VMEM((UNITS, HALF), bf16),
            pltpu.VMEM((HALF, 512), bf16),
            pltpu.VMEM((REQ, 4 * CTX_DEV, HD), bf16),
            pltpu.VMEM((REQ, HD, 4 * CTX_DEV), bf16),
            pltpu.VMEM((REQ, 4 * CTX_DEV, HD), bf16),
            pltpu.VMEM((2, REQ, HD), bf16),
            pltpu.VMEM((PEERS, REQ, HD), bf16),
            pltpu.VMEM((KV_PEERS, REQ, HD), bf16),
            pltpu.VMEM((HEADS * REQ, HD), f32),
            pltpu.VMEM((HEADS * 16, HD), f32),
            pltpu.VMEM((HEADS, 16, HD), bf16),
            pltpu.VMEM((PEERS, 16, HD), bf16),
            pltpu.VMEM((PEERS, 4, HD), f32),
            pltpu.VMEM((PEERS, 4, HD), f32),
            pltpu.VMEM((PEERS, 4, HD), f32),
            pltpu.VMEM((2, REQ, 256), f32),
            pltpu.VMEM((2, REQ, 256), f32),
            pltpu.VMEM((PEERS, 4, HD), f32),
            pltpu.VMEM((PEERS, 4, HD), f32),
            pltpu.VMEM((REQ, HALF), bf16),
            pltpu.SemaphoreType.DMA((12,)),
            pltpu.SemaphoreType.DMA((2 * REQ,)),
            pltpu.SemaphoreType.DMA((7,)),
            pltpu.SemaphoreType.DMA((7,)),
        ],
        compiler_params=pltpu.CompilerParams(
            collective_id=0, has_side_effects=True, vmem_limit_bytes=60 << 20
        ),
    )(
        hidden_states,
        attn_gain.reshape(1, WIDTH),
        ffn_gain.reshape(1, WIDTH),
        w_query.reshape(HALF, HD),
        w_keyval.reshape(HALF, 32).T,
        w_out.reshape(HD, HALF),
        w_gate.T,
        w_up.T,
        w_down,
        kv_cache,
        lengths,
        first_shard,
    )


def solution(mesh):
    placed = (
        P(),
        P(),
        P(),
        P("grp", "rep", "tp", None),
        P("grp", "rep", "tp"),
        P("rep", "tp", None, "grp"),
        P("grp", ("tp", "rep")),
        P("grp", ("tp", "rep")),
        P(("tp", "rep"), "grp"),
        P(None, ("grp", "tp"), "rep", None),
        P(),
        P(),
    )
    return jax.shard_map(
        on_device,
        mesh=mesh,
        in_specs=placed,
        out_specs=P(None, ("grp", "tp", "rep")),
        check_vma=False,
    )
```

```python
import functools
import math

import numpy as np
import jax
import jax.numpy as jnp
from jax import lax
from jax.sharding import PartitionSpec as P
import jax.experimental.pallas as pl
import jax.experimental.pallas.tpu as pltpu

MESH = pl.DeviceIdType.MESH
NT = (((1,), (1,)), ((), ()))
epsilon = 1e-05
base_freq = 500000.0
masked = -1e30
floor_peak = -1e20

REQ = 8
WIDTH = 8192
HALF = WIDTH // 2
TILES = HALF // 128
HD = 128
CTX_DEV = 512
HEADS = 32
N_TP = 32
PEERS = 64
UNITS = 224
FREQ = [
    float(f)
    for f in (base_freq ** (-(2.0 * np.arange(HD // 2, dtype=np.float64)) / HD)).astype(np.float32)
]


def swap_halves(tile, diagonal):
    turned = pltpu.roll(pltpu.roll(tile, 64, 1), 4, 0)
    return jnp.where(diagonal, tile, turned)


def layer(
    hidden_ref, attn_gain_ref, ffn_gain_ref, wq_ref, wkv_ref, wo_ref, wg_ref, wu_ref, wd_ref,
    kv_ref, lengths_ref, first_shard_ref, out_ref,
    len_ref, first_ref, hid, gain_a, gain_f, wq, wkv, wo, wg, wu, wd, w_in, keys, keys_t, values,
    send_a, recv_a, q_rot, stage_c, send_c, recv_c, send_d, recv_d, recv_e, send_f, recv_f,
    send_g, recv_g, x_ffn, load_sem, kv_sem, send_sem, recv_sem,
):
    g = lax.axis_index("grp")
    t = lax.axis_index("tp")
    r = lax.axis_index("rep")
    me_row = g * N_TP + t
    me_col = t * 2 + r

    y, x, z = me_row // 16, (t // 4) % 4, t % 4

    def far_first(i):
        return 2 + i - (i // 2) * (2 * i - 1)

    def row_peer(k):
        there = lax.rem(me_row + 1 + k, PEERS)
        return there, (lax.div(there, N_TP), lax.rem(there, N_TP), r)

    def col_peer(k):
        there = lax.rem(me_col + 1 + k, PEERS)
        return there, (g, lax.div(there, 2), lax.rem(there, 2))

    barrier = pltpu.get_barrier_semaphore()

    @pl.loop(0, PEERS - 1, unroll=9)
    def _(k):
        _, dev = row_peer(k)
        pl.semaphore_signal(barrier, inc=1, device_id=dev, device_id_type=MESH)

    pl.semaphore_signal(barrier, inc=1, device_id=(g, t, 1 - r), device_id_type=MESH)

    own_half = pl.ds(pl.multiple_of(g * HALF, HALF), HALF)
    other_half = pl.ds(pl.multiple_of((1 - g) * HALF, HALF), HALF)
    loads = [
        (hidden_ref.at[:, own_half], hid.at[0]),
        (hidden_ref.at[:, other_half], hid.at[1]),
        (attn_gain_ref.at[:, own_half], gain_a),
        (wq_ref, wq),
        (wkv_ref, wkv),
        (ffn_gain_ref.at[:, own_half], gain_f),
        (wo_ref, wo),
        (wg_ref, wg),
        (wu_ref, wu),
        (wd_ref, wd),
        (lengths_ref, len_ref),
        (first_shard_ref, first_ref),
    ]
    copies = [pltpu.make_async_copy(s, d, load_sem.at[i]) for i, (s, d) in enumerate(loads)]
    kv_rows = kv_ref.reshape(REQ, 4 * CTX_DEV, 2 * HD)
    kv_copies = []
    for b in range(REQ):
        for i, dst in enumerate((keys, values)):
            kv_copies.append(
                pltpu.make_async_copy(
                    kv_rows.at[b, :, pl.ds(i * HD, HD)], dst.at[b], kv_sem.at[2 * b + i]
                )
            )
    for c in copies[:5] + copies[10:]:
        c.start()

    for c in copies[:5]:
        c.wait()
    for c in kv_copies[::2] + kv_copies[1::2] + copies[5:10]:
        c.start()
    own = hid[0].astype(jnp.float32)
    other = hid[1].astype(jnp.float32)
    squares = jnp.sum(own * own, axis=1, keepdims=True) + jnp.sum(
        other * other, axis=1, keepdims=True
    )
    scale = lax.rsqrt(squares * (1.0 / WIDTH) + epsilon)
    normed = (own * scale * gain_a[...]).astype(jnp.bfloat16)
    query_part = jnp.dot(normed, wq[...], preferred_element_type=jnp.float32)
    keyval_part = lax.dot_general(normed, wkv[...], NT, preferred_element_type=jnp.float32)
    keyval_wide = jnp.concatenate(
        (keyval_part, jnp.zeros((REQ, HD - 32), jnp.float32)), axis=1
    )
    spot = t % 4
    placed = keyval_wide
    for s in range(1, 4):
        placed = jnp.where(spot == s, pltpu.roll(keyval_wide, 32 * s, 1), placed)
    message = jnp.concatenate((query_part, placed), axis=0).astype(jnp.bfloat16)
    send_a[...] = message
    recv_a[me_row] = message

    pl.semaphore_wait(barrier, PEERS)

    def send_all(peer, source, landing, stage):
        @pl.loop(0, PEERS - 1, unroll=9)
        def _(k):
            p, dev = peer(k)
            pltpu.make_async_remote_copy(
                src_ref=source(p),
                dst_ref=landing,
                send_sem=send_sem.at[stage],
                recv_sem=recv_sem.at[stage],
                device_id=dev,
                device_id_type=MESH,
            ).start()

    def wait_all(buffer, sem):
        span = buffer.at[pl.ds(0, PEERS - 1)]
        pltpu.make_async_copy(span, span, sem).wait()

    send_all(row_peer, lambda p: send_a, recv_a.at[me_row], 0)

    lane8 = lax.broadcasted_iota(jnp.int32, (REQ, HD), 1)
    row8 = lax.broadcasted_iota(jnp.int32, (REQ, HD), 0)
    frequency = jnp.zeros((REQ, HD), jnp.float32)
    for i in range(HD // 2):
        frequency = jnp.where(lane8 // 2 == i, FREQ[i], frequency)
    position = jnp.zeros((REQ, HD), jnp.int32)
    for c in copies[10:]:
        c.wait()
    for b in range(REQ):
        position = jnp.where(row8 == b, len_ref[b], position)
    angles = position.astype(jnp.float32) * frequency
    cos_part = jnp.cos(angles)
    sin_part = jnp.sin(angles)
    even = lane8 % 2 == 0
    sin_even = jnp.where(even, -sin_part, 0.0)
    sin_odd = jnp.where(even, 0.0, sin_part)

    def rotate(x):
        return (
            x * cos_part + pltpu.roll(x, HD - 1, 1) * sin_even + pltpu.roll(x, 1, 1) * sin_odd
        )

    rounded = lambda x: x.astype(jnp.bfloat16).astype(jnp.float32)
    lane_row = lax.broadcasted_iota(jnp.int32, (REQ, 4 * CTX_DEV), 1)
    of_kv_head = [lane_row % 4 == i for i in range(4)]
    quarter = lane8 // 32
    diagonal = (lane8 < 64) == (row8 < 4)
    inv_scale = 1.0 / math.sqrt(HD)

    for b in range(REQ):
        kv_copies[2 * b].wait()
        keys_t[b] = keys[b].T

    wait_all(recv_a, recv_sem.at[0])
    for head in range(HEADS):
        pair = recv_a[head].astype(jnp.float32) + recv_a[N_TP + head].astype(jnp.float32)
        q_rot[pl.ds(head * REQ, REQ), :] = rounded(rotate(rounded(pair[:REQ])))

    def spread(row, op):
        for shift in (4, 8, 16, 32, 64):
            row = op(row, pltpu.roll(row, shift, 1))
        return row

    scores = []
    for b in range(REQ):
        q_b = q_rot[pl.ds(b, HEADS, stride=REQ), :].astype(jnp.bfloat16)
        scores.append(jnp.dot(q_b, keys_t[b], preferred_element_type=jnp.float32))
    weights = []
    for b in range(REQ):
        block = (me_row - first_ref[b]) & (PEERS - 1)
        live_rows = 4 * (len_ref[b] - block * CTX_DEV)
        grid = [scores[b][8 * i : 8 * i + 8] for i in range(4)]
        score = jnp.where(
            of_kv_head[0],
            grid[0],
            jnp.where(of_kv_head[1], grid[1], jnp.where(of_kv_head[2], grid[2], grid[3])),
        )
        score = jnp.where(lane_row < live_rows, score * inv_scale, masked)
        peak = functools.reduce(
            jnp.maximum, [score[:, HD * i : HD * i + HD] for i in range(4 * CTX_DEV // HD)]
        )
        peak = jnp.maximum(spread(peak, jnp.maximum), floor_peak)
        peak_hi = rounded(peak)
        peak_lo = rounded(peak - peak_hi)
        base = peak_hi + peak_lo
        weight = jnp.exp(score - jnp.concatenate([base] * (4 * CTX_DEV // HD), axis=1))
        total = functools.reduce(
            jnp.add, [weight[:, HD * i : HD * i + HD] for i in range(4 * CTX_DEV // HD)]
        )
        total = spread(total, jnp.add)
        total_hi = rounded(total)
        total_lo = rounded(total - total_hi)
        stats = jnp.where(
            quarter < 2,
            jnp.where(quarter == 0, peak_hi, peak_lo),
            jnp.where(quarter == 2, total_hi, total_lo),
        )
        for i in range(4):
            stage_c[pl.ds(REQ + b + 16 * 8 * i, 8, stride=16), :] = stats
        weights.append(
            jnp.concatenate(
                [jnp.where(of_kv_head[i], weight, 0.0) for i in range(4)], axis=0
            ).astype(jnp.bfloat16)
        )
    for b in range(REQ):
        kv_copies[2 * b + 1].wait()
    for b in range(REQ):
        stage_c[pl.ds(b, HEADS, stride=16), :] = jnp.dot(
            weights[b], values[b], preferred_element_type=jnp.float32
        )
    for head in range(HEADS):
        send_c[head] = stage_c[pl.ds(head * 16, 16), :].astype(jnp.bfloat16)
    recv_c[me_row] = send_c[t]
    send_all(row_peer, lambda p: send_c.at[lax.rem(p, N_TP)], recv_c.at[me_row], 1)

    for c in copies[7:9]:
        c.wait()
    for first in (UNITS, 256 + UNITS):
        w_in[:, first : first + 256 - UNITS] = jnp.zeros((HALF, 256 - UNITS), jnp.bfloat16)
    w_in[:, :UNITS] = wg[...].T
    w_in[:, 256 : 256 + UNITS] = wu[...].T
    kv_first = (t // 8) * 8
    new_key = jnp.zeros((REQ, HD), jnp.float32)
    new_value = jnp.zeros((REQ, HD), jnp.float32)
    for j in range(4):
        part = recv_a[kv_first + j].astype(jnp.float32) + recv_a[N_TP + kv_first + j].astype(
            jnp.float32
        )
        new_key = new_key + part[REQ:]
        part = recv_a[kv_first + 4 + j].astype(jnp.float32) + recv_a[
            N_TP + kv_first + 4 + j
        ].astype(jnp.float32)
        new_value = new_value + part[REQ:]
    key_rot = rounded(rotate(rounded(new_key)))
    new_value = rounded(new_value)
    my_query = q_rot[pl.ds(pl.multiple_of(t * REQ, REQ), REQ), :]
    own_score = jnp.sum(my_query * key_rot, axis=1, keepdims=True) * inv_scale
    pick_row = lax.broadcasted_iota(jnp.int32, (HD, 2 * HD), 0)
    pick_col = lax.broadcasted_iota(jnp.int32, (HD, 2 * HD), 1)
    pick = jnp.where(
        (pick_row % 32 == t // 8) & (pick_row // 64 == pick_col // HD), 1.0, 0.0
    ).astype(jnp.bfloat16)

    wait_all(recv_c, recv_sem.at[1])
    partial = recv_c[...]
    stats_all = partial.astype(jnp.float32)[:, REQ:, :].reshape(PEERS * REQ, HD).astype(jnp.bfloat16)
    spread = jnp.dot(stats_all, pick, preferred_element_type=jnp.float32)
    peaks = spread[:, :HD].reshape(PEERS, REQ, HD)
    totals = spread[:, HD:].reshape(PEERS, REQ, HD)
    top = jnp.maximum(jnp.max(peaks, axis=0), own_score)
    keep = jnp.exp(peaks - top[None])
    own_weight = jnp.exp(own_score - top)
    numer = jnp.sum(keep * partial.astype(jnp.float32)[:, :REQ, :], axis=0)
    denom = jnp.sum(keep * totals, axis=0) + own_weight
    attended = ((numer + rounded(own_weight) * new_value) / denom).astype(jnp.bfloat16)

    def scatter(send, recv, row, weight, stage):
        for i in range(TILES // 2):
            product = jnp.dot(
                row, weight[:, pl.ds(i * 256, 256)], preferred_element_type=jnp.float32
            )
            for j in range(2):
                tile = swap_halves(product[:, j * 128 : j * 128 + 128], diagonal)
                send[4 * i + 2 * j] = tile[:4]
                send[4 * i + 2 * j + 1] = tile[4:]
        recv[me_col] = send[me_col]
        send_all(col_peer, lambda p: send.at[p], recv.at[me_col], stage)

    copies[6].wait()
    scatter(send_d, recv_d, attended, wo, 2)
    my_column = pl.ds(pl.multiple_of(t * 128, 128), 128)
    my_hidden = swap_halves(hid[0, :, my_column].astype(jnp.float32), diagonal)
    my_hidden = jnp.where(r == 0, my_hidden[:4], my_hidden[4:])
    wait_all(recv_d, recv_sem.at[2])
    projected = jnp.sum(recv_d[...], axis=0)
    recv_e[me_col] = projected
    send_all(col_peer, lambda p: recv_e.at[me_col], recv_e.at[me_col], 3)
    my_middle = rounded(my_hidden + projected)
    for c in copies[5:6] + copies[9:10]:
        c.wait()
    wait_all(recv_e, recv_sem.at[3])
    squares = jnp.zeros((REQ, HD), jnp.float32)
    for i in range(TILES):
        packed = jnp.concatenate((recv_e[2 * i], recv_e[2 * i + 1]), axis=0)
        col = pl.ds(i * 128, 128)
        middle = rounded(hid[0, :, col].astype(jnp.float32) + swap_halves(packed, diagonal))
        squares = squares + middle * middle
        x_ffn[:, col] = (middle * gain_f[:, col]).astype(jnp.bfloat16)

    product = jnp.dot(x_ffn[...], w_in[...], preferred_element_type=jnp.float32)
    gate_part = product[:, :UNITS]
    up_part = product[:, 256 : 256 + UNITS]
    square_sum = jnp.broadcast_to(jnp.sum(squares, axis=1, keepdims=True), (REQ, 256 - UNITS))
    send_f[0] = jnp.concatenate((gate_part, square_sum), axis=1)
    send_f[1] = jnp.concatenate((up_part, square_sum), axis=1)
    swap = pltpu.make_async_remote_copy(
        src_ref=send_f,
        dst_ref=recv_f,
        send_sem=send_sem.at[4],
        recv_sem=recv_sem.at[4],
        device_id=(1 - g, t, r),
        device_id_type=MESH,
    )
    swap.start()
    swap.wait_recv()
    gate_sum = send_f[0] + recv_f[0]
    up_sum = send_f[1] + recv_f[1]
    scale = lax.rsqrt(gate_sum[:, UNITS : UNITS + 1] * (1.0 / WIDTH) + epsilon)
    gate = gate_sum[:, :UNITS] * scale
    up = up_sum[:, :UNITS] * scale
    active = (gate / (1.0 + jnp.exp(-gate)) * up).astype(jnp.bfloat16)

    scatter(send_g, recv_g, active, wd, 5)
    wait_all(recv_g, recv_sem.at[5])
    result = my_middle + jnp.sum(recv_g[...], axis=0)
    out_ref[...] = jnp.concatenate((result[:, :64], result[:, 64:]), axis=0).astype(out_ref.dtype)

    wait_all(recv_a, send_sem.at[0])
    wait_all(recv_c, send_sem.at[1])
    wait_all(recv_d, send_sem.at[2])
    wait_all(recv_e, send_sem.at[3])
    swap.wait_send()
    wait_all(recv_g, send_sem.at[5])


def on_device(
    hidden_states, attn_gain, ffn_gain, w_query, w_keyval, w_out, w_gate, w_up, w_down,
    kv_cache, lengths, first_shard,
):
    outside = pl.BlockSpec(memory_space=pltpu.HBM)
    f32, bf16 = jnp.float32, jnp.bfloat16
    return pl.pallas_call(
        layer,
        out_shape=jax.ShapeDtypeStruct((REQ, 64), bf16),
        in_specs=[outside] * 12,
        out_specs=pl.BlockSpec(memory_space=pltpu.VMEM),
        scratch_shapes=[
            pltpu.SMEM((REQ,), jnp.int32),
            pltpu.SMEM((REQ,), jnp.int32),
            pltpu.VMEM((2, REQ, HALF), bf16),
            pltpu.VMEM((1, HALF), f32),
            pltpu.VMEM((1, HALF), f32),
            pltpu.VMEM((HALF, HD), bf16),
            pltpu.VMEM((32, HALF), bf16),
            pltpu.VMEM((HD, HALF), bf16),
            pltpu.VMEM((UNITS, HALF), bf16),
            pltpu.VMEM((UNITS, HALF), bf16),
            pltpu.VMEM((UNITS, HALF), bf16),
            pltpu.VMEM((HALF, 512), bf16),
            pltpu.VMEM((REQ, 4 * CTX_DEV, HD), bf16),
            pltpu.VMEM((REQ, HD, 4 * CTX_DEV), bf16),
            pltpu.VMEM((REQ, 4 * CTX_DEV, HD), bf16),
            pltpu.VMEM((16, HD), bf16),
            pltpu.VMEM((PEERS, 16, HD), bf16),
            pltpu.VMEM((HEADS * REQ, HD), f32),
            pltpu.VMEM((HEADS * 16, HD), f32),
            pltpu.VMEM((HEADS, 16, HD), bf16),
            pltpu.VMEM((PEERS, 16, HD), bf16),
            pltpu.VMEM((PEERS, 4, HD), f32),
            pltpu.VMEM((PEERS, 4, HD), f32),
            pltpu.VMEM((PEERS, 4, HD), f32),
            pltpu.VMEM((2, REQ, 256), f32),
            pltpu.VMEM((2, REQ, 256), f32),
            pltpu.VMEM((PEERS, 4, HD), f32),
            pltpu.VMEM((PEERS, 4, HD), f32),
            pltpu.VMEM((REQ, HALF), bf16),
            pltpu.SemaphoreType.DMA((12,)),
            pltpu.SemaphoreType.DMA((2 * REQ,)),
            pltpu.SemaphoreType.DMA((6,)),
            pltpu.SemaphoreType.DMA((6,)),
        ],
        compiler_params=pltpu.CompilerParams(
            collective_id=0, has_side_effects=True, vmem_limit_bytes=60 << 20
        ),
    )(
        hidden_states,
        attn_gain.reshape(1, WIDTH),
        ffn_gain.reshape(1, WIDTH),
        w_query.reshape(HALF, HD),
        w_keyval.reshape(HALF, 32).T,
        w_out.reshape(HD, HALF),
        w_gate.T,
        w_up.T,
        w_down,
        kv_cache,
        lengths,
        first_shard,
    )


def solution(mesh):
    placed = (
        P(),
        P(),
        P(),
        P("grp", "rep", "tp", None),
        P("grp", "rep", "tp"),
        P("rep", "tp", None, "grp"),
        P("grp", ("tp", "rep")),
        P("grp", ("tp", "rep")),
        P(("tp", "rep"), "grp"),
        P(None, ("grp", "tp"), "rep", None),
        P(),
        P(),
    )
    return jax.shard_map(
        on_device,
        mesh=mesh,
        in_specs=placed,
        out_specs=P(None, ("grp", "tp", "rep")),
        check_vma=False,
    )
```
